32 devices in a mesh: groups: 2 (over y), seq: 4 (over z), tp: 2 (over x), kvh: 2 (over core).
Axes of the slice: x: 2, y: 2, z: 4, core: 2. Of those that a mesh axis runs over, the one named last changes fastest.
Arguments:
- pool_kv: bfloat16 [16, 2, 256, 512], P(('groups', 'seq'), None, None, ('tp', 'kvh')), parts along dimension 0, may hold values from -24 to 24
- hidden_rows: bfloat16 [16, 40, 4096], P(('groups', 'seq'), None, ('tp', 'kvh')), parts along dimension 0, may hold values from -512 to 512
- norm_gain: bfloat16 [4096], P(('tp', 'kvh')), may hold values from 0.099609375 to 1.8984375
- kv_weight: bfloat16 [4096, 1024], P(('tp', 'kvh')), may hold values from -0.09375 to 0.09375
- queries: bfloat16 [16, 40, 4096], P(('groups', 'seq'), None, ('tp', 'kvh')), parts along dimension 0, may hold values from -64 to 64
- stretch_slot: int32 [8], P('groups'), parts along dimension 0, may hold values from 0 to 7, as said below
- stretch_lengths: int32 [8], P('groups'), parts along dimension 0, may hold values from 128 to 256
- recompute_rows: int32 [16, 40], P(('groups', 'seq')), parts along dimension 0, may hold values from 0 to 255, as said below
Outputs:
- fresh_kv: bfloat16 [16, 2, 40, 512], P(('groups', 'seq'), None, None, ('tp', 'kvh')), parts along dimension 0
- attended: bfloat16 [16, 40, 4096], P(('groups', 'seq'), None, ('tp', 'kvh')), parts along dimension 0
The draws below stay inside these ranges and needn't reach their ends.
There are 2 independent parts, one for each index of `groups`. The reference program is written for one: setup_inputs(seed, part) draws one part's arguments, and reference() takes and returns one part's arrays. A program takes and returns all parts, laid end to end along the dimension named above; an argument that names none is the same for every part. Nothing has to cross between parts.
Inputs may be any that keep to these rules, and one draw needn't show every extreme that they name: `stretch_slot`: distinct pool slots; slot s lies with owner s // 2 along seq. `recompute_rows`: each row distinct and ascending, below the length of the stretch that the slot holds, and below 128 in a slot that holds none.
All inputs are finite; a program needn't handle non-finite values.
Results may differ from the reference program's by a relative error of at most 0.011.
Values may be sent and summed in bfloat16 or wider, within the bound.
No kernel may reach another device: no remote copies, remote signals or barrier semaphores. Data moves between devices by JAX's collectives and lax.ppermute only.
A program may use at most 128 MiB of HBM per device.

```python
import jax
import jax.numpy as jnp
from jax import lax

D = 4096
HD = 128
GROUP = 8
CH = 256
R = 40
KVH = 4
POS = 4
POOL = 8


def layout_draw(key):
    keys_all = jax.random.split(key, 5)
    inner = 1 + jax.random.permutation(keys_all[0], POOL - 2)[:POS - 2]
    chosen = jnp.concatenate([jnp.array([0, POOL - 1], jnp.int32), inner.astype(jnp.int32)])
    slots_map = chosen[jax.random.permutation(keys_all[1], POS)]
    lengths_map = jax.random.randint(keys_all[2], (POS,), CH // 2, CH + 1)
    longest = jax.random.randint(keys_all[3], (), 0, POS)
    shortest = (longest + 1 + jax.random.randint(keys_all[4], (), 0, POS - 1)) % POS
    places = jnp.arange(POS)
    lengths_map = jnp.where(places == longest, CH, jnp.where(places == shortest, CH // 2, lengths_map))
    return (slots_map.astype(jnp.int32), lengths_map.astype(jnp.int32))


def draw_stretch_slot(key, part):
    slots_map, lengths_map = layout_draw(key)
    return slots_map


def draw_stretch_lengths(key, part):
    slots_map, lengths_map = layout_draw(key)
    return lengths_map


def draw_recompute_rows(key, part):
    slots_map, lengths_map = layout_draw(key)
    key = jax.random.fold_in(key, 3)
    hits = slots_map[:, None] == jnp.arange(POOL, dtype=jnp.int32)[None, :]
    held = jnp.any(hits, 0)
    slot_len = jnp.where(held, jnp.sum(jnp.where(hits, lengths_map[:, None], 0), 0), CH // 2)
    places = jnp.arange(CH, dtype=jnp.int32)[None, :]
    scores = jax.random.randint(key, (POOL, CH), 0, 1 << 20) * CH + places
    scores = jnp.where((slot_len[:, None] == CH) & (places == CH - 1), 1 << 30, scores)
    scores = jnp.where(held[:, None] & (slot_len[:, None] == CH // 2) & (places == 0), 1 << 30, scores)
    scores = jnp.where(places < slot_len[:, None], scores, -1 - places)
    picked = lax.top_k(scores, R)[1]
    return jnp.sort(picked, axis=1).astype(jnp.int32)


def draw_pool_kv(key, part):
    key = jax.random.fold_in(key, 5)
    first_key = jax.random.fold_in(key, 0)
    shape = (POOL, 2, CH, KVH * HD)
    values = jnp.clip(jax.random.normal(first_key, shape, jnp.float32), -6.0, 6.0)
    return values.astype(jnp.bfloat16)


def draw_queries(key, part):
    key = jax.random.fold_in(key, 9)
    first_key = jax.random.fold_in(key, 0)
    shape = (POOL, R, KVH * GROUP * HD)
    values = jnp.clip(jax.random.normal(first_key, shape, jnp.float32), -6.0, 6.0)
    return values.astype(jnp.bfloat16)


def draw_hidden_rows(key, part):
    key = jax.random.fold_in(key, 7)
    keys_all = jax.random.split(key, 2)
    shape = (POOL, R, D)
    column = 10.0 ** (lax.broadcasted_iota(jnp.float32, (1, 1, D), 2) / (D - 1))
    values = jnp.clip(jax.random.normal(keys_all[0], shape, jnp.float32), -4.0, 4.0)
    row_scale = 10.0 ** jax.random.uniform(keys_all[1], (POOL, R, 1), jnp.float32, 0.0, 1.0)
    return (values * column * row_scale).astype(jnp.bfloat16)


def block_scale(rng, shape, pieces, least, largest):
    def one(axis_at, parts):
        heights = jax.random.uniform(jax.random.fold_in(jax.random.fold_in(rng, 6), axis_at), (parts,), jnp.float32, least / len(pieces), largest / len(pieces))
        return jnp.repeat(jnp.exp(heights), shape[axis_at] // parts).reshape((-1,) + (1,) * (len(shape) - axis_at - 1))

    gain = one(*pieces[0])
    for cut in pieces[1:]:
        gain = gain * one(*cut)
    return gain


def scatter_about(key, shape, spread, limit, cuts=(), kind=jnp.bfloat16):
    factor_of = block_scale(key, shape, cuts, -0.22, 0.18) if cuts else 1.0
    values = jax.random.normal(key, shape, jnp.float32) * spread * factor_of
    return jnp.minimum(jnp.maximum(values, -limit), limit).astype(kind)


def setup_inputs(seed: int = 0, part: int = 0) -> dict:
    splits = jax.random.split(jax.random.key(seed), 9)
    part_splits = jax.random.split(jax.random.fold_in(splits[8], part), 9)
    pool_kv = draw_pool_kv(jax.random.fold_in(jax.random.fold_in(splits[8], part), 71), part)
    hidden_rows = draw_hidden_rows(jax.random.fold_in(jax.random.fold_in(splits[8], part), 71), part)
    norm_gain = jnp.clip(1.0 + 0.18 * jax.random.normal(splits[2], (D,), jnp.float32), 0.099609375, 1.8984375).astype(jnp.bfloat16)
    kv_weight = scatter_about(splits[3], (D, 2 * KVH * HD), D ** -0.5, 0.09375, ((0, 4),))
    queries = draw_queries(jax.random.fold_in(jax.random.fold_in(splits[8], part), 71), part)
    stretch_slot = draw_stretch_slot(jax.random.fold_in(jax.random.fold_in(splits[8], part), 71), part)
    stretch_lengths = draw_stretch_lengths(jax.random.fold_in(jax.random.fold_in(splits[8], part), 71), part)
    recompute_rows = draw_recompute_rows(jax.random.fold_in(jax.random.fold_in(splits[8], part), 71), part)
    return {"pool_kv": pool_kv, "hidden_rows": hidden_rows, "norm_gain": norm_gain, "kv_weight": kv_weight, "queries": queries, "stretch_slot": stretch_slot, "stretch_lengths": stretch_lengths, "recompute_rows": recompute_rows}


THETA = 500000.0

def rotate(values, positions):
    half = values.shape[-1] // 2
    inverse = THETA ** (-(jnp.arange(half, dtype=jnp.float32) * 2.0) / values.shape[-1])
    angle = positions.astype(jnp.float32)[..., None] * inverse
    cosine = jnp.cos(angle)
    sine = jnp.sin(angle)
    first = values[..., :half]
    second = values[..., half:]
    return jnp.concatenate([first * cosine - second * sine, second * cosine + first * sine], -1)

def reference(pool_kv, hidden_rows, norm_gain, kv_weight, queries, stretch_slot, stretch_lengths, recompute_rows):
    slot_ids = jnp.arange(POOL, dtype=jnp.int32)
    hits = stretch_slot[:, None] == slot_ids[None, :]
    held = jnp.any(hits, 0)
    slot_position = jnp.where(held, lax.optimization_barrier(jnp.sum(jnp.where(hits, jnp.arange(POS, dtype=jnp.int32)[:, None], 0), 0)), -1).astype(jnp.int32)
    slot_length = lax.optimization_barrier(jnp.sum(jnp.where(hits, stretch_lengths[:, None], 0), 0)).astype(jnp.int32)
    inputs = hidden_rows.astype(jnp.float32)
    mean_sq = lax.optimization_barrier(jnp.mean(inputs * inputs, -1, keepdims=True))
    normed = (inputs * lax.rsqrt(mean_sq + 1e-05) * norm_gain.astype(jnp.float32)).astype(jnp.bfloat16)
    fresh_flat = jnp.dot(normed.reshape(POOL * R, D), kv_weight, preferred_element_type=jnp.float32).astype(jnp.bfloat16)
    fresh_kv = fresh_flat.reshape(POOL, R, KVH, 2, HD).transpose(0, 3, 1, 2, 4).reshape(POOL, 2, R, KVH * HD)

    def patch_slot(cached, rows_here, fresh_here):
        return cached.at[:, rows_here, :].set(fresh_here)
    patched = jax.vmap(patch_slot)(pool_kv, recompute_rows, fresh_kv)
    token_ids = jnp.arange(CH, dtype=jnp.int32)
    key_pos = slot_position[:, None] * CH + token_ids[None, :]
    key_rows = patched[:, 0].reshape(POOL, CH, KVH, HD).astype(jnp.float32)
    rotated_keys = rotate(key_rows, key_pos[:, :, None]).astype(jnp.bfloat16)
    value_rows = patched[:, 1].reshape(POOL, CH, KVH, HD)
    query_pos = slot_position[:, None] * CH + recompute_rows
    query_rows = queries.reshape(POOL, R, KVH, GROUP, HD).astype(jnp.float32)
    rotated_queries = rotate(query_rows, query_pos[:, :, None, None]).astype(jnp.bfloat16)
    keys_flat = rotated_keys.reshape(POOL * CH, KVH, HD).astype(jnp.float32)
    values_flat = value_rows.reshape(POOL * CH, KVH, HD).astype(jnp.float32)
    key_pos_flat = key_pos.reshape(POOL * CH)
    key_valid = ((slot_position[:, None] >= 0) & (token_ids[None, :] < slot_length[:, None])).reshape(POOL * CH)
    scale = HD ** (-0.5)

    def one_slot(operands):
        query_here, position_here, valid_here = operands
        scores = jnp.einsum('rhgd,khd->hrgk', query_here.astype(jnp.float32), keys_flat) * scale
        visible = key_valid[None, None, None, :] & (key_pos_flat[None, None, None, :] <= position_here[None, :, None, None])
        masked = jnp.where(visible, scores, -1e+30)
        highest = lax.optimization_barrier(jnp.max(masked, -1, keepdims=True))
        weight = jnp.where(visible, jnp.exp(masked - highest), 0.0)
        denom = lax.optimization_barrier(jnp.sum(weight, -1))
        prob = weight.astype(jnp.bfloat16).astype(jnp.float32)
        numer = jnp.einsum('hrgk,khd->hrgd', prob, values_flat)
        result = numer / jnp.where(denom > 0, denom, 1.0)[..., None]
        result = jnp.where(valid_here, result, 0.0)
        return result.transpose(1, 0, 2, 3).astype(jnp.bfloat16)
    outputs = lax.map(one_slot, (rotated_queries, query_pos, slot_position >= 0))
    attended = outputs.reshape(POOL, R, KVH * GROUP * HD)
    return (fresh_kv, attended)
```

```python
import functools
import math

import jax
import jax.numpy as jnp
import numpy as np
from jax import lax
from jax.experimental import pallas as pl
from jax.experimental.pallas import tpu as pltpu
from jax.sharding import PartitionSpec as P

THETA = 500000.0
EPS = 1e-05
FAR = -1e30
FEATURES = ("tp", "kvh")
VMEM = pltpu.MemorySpace.VMEM
SMEM = pltpu.MemorySpace.SMEM


def round_up(value, step):
    return -(-value // step) * step


def rope_tables(positions, width):
    inverse = THETA ** (-2.0 * np.arange(width // 2) / width)
    angle = np.asarray(positions, np.float64)[:, None] * np.concatenate([inverse, inverse])[None]
    return np.cos(angle).astype(np.float32), np.sin(angle).astype(np.float32)


def turn(values, cosine, sine):
    return values * cosine + pltpu.roll(values, values.shape[-1] // 2, 1) * sine


def project_body(me_ref, hidden_ref, gain_ref, weight_ref, *refs):
    del me_ref
    pieces, scaled, tail = refs[:-2], refs[-2], refs[-1]
    step = pl.program_id(0)
    count = scaled.shape[0]
    spare = tail.shape[0]

    @pl.when(step == 0)
    def _():
        hidden = hidden_ref[...].astype(jnp.float32).reshape(count, -1)
        scaled[...] = (hidden * gain_ref[...].astype(jnp.float32)).astype(jnp.bfloat16)
        square = hidden * hidden
        fill = jnp.zeros((round_up(count, 128) - count, square.shape[1]), jnp.float32)
        square = jnp.concatenate([square, fill], 0)
        high = square.astype(jnp.bfloat16)
        low = (square - high.astype(jnp.float32)).astype(jnp.bfloat16)
        ones = jnp.ones((spare, square.shape[1]), jnp.bfloat16)
        along = (((1,), (1,)), ((), ()))
        total = lax.dot_general(ones, high, along, preferred_element_type=jnp.float32)
        total += lax.dot_general(ones, low, along, preferred_element_type=jnp.float32)
        coarse = total.astype(jnp.bfloat16).astype(jnp.float32)
        row = lax.broadcasted_iota(jnp.int32, total.shape, 0)
        both = jnp.where(row == 0, coarse, jnp.where(row == 1, total - coarse, 0.0))
        rest = jnp.zeros((spare, tail.shape[1] - total.shape[1]), jnp.float32)
        tail[...] = jnp.concatenate([both, rest], 1)

    product = jnp.dot(scaled[...], weight_ref[...], preferred_element_type=jnp.float32)
    product = jnp.concatenate([product, tail[...]], 0).astype(jnp.bfloat16)
    for at, piece in enumerate(pieces):

        @pl.when(step == at)
        def _(piece=piece):
            piece[...] = product


def project(me, hidden_rows, norm_gain, kv_weight, parts):
    slots, rows, features = hidden_rows.shape
    count = slots * rows
    columns = kv_weight.shape[1] // parts
    shape = (count + 16, columns)
    return pl.pallas_call(
        project_body,
        out_shape=[jax.ShapeDtypeStruct(shape, jnp.bfloat16)] * parts,
        grid_spec=pltpu.PrefetchScalarGridSpec(
            num_scalar_prefetch=1,
            grid=(parts,),
            in_specs=[
                pl.BlockSpec((slots, rows, features), lambda k, me: (0, 0, 0)),
                pl.BlockSpec((1, features), lambda k, me: (0, 0)),
                pl.BlockSpec((features, columns), lambda k, me: (0, me[0] ^ k)),
            ],
            out_specs=[pl.BlockSpec(shape, lambda k, me: (0, 0))] * parts,
            scratch_shapes=[
                pltpu.VMEM((count, features), jnp.bfloat16),
                pltpu.VMEM((16, columns), jnp.float32),
            ],
        ),
        cost_estimate=pl.CostEstimate(flops=1000, bytes_accessed=1000, transcendentals=0),
        compiler_params=pltpu.CompilerParams(vmem_limit_bytes=48 << 20),
        name="project",
    )(me, hidden_rows, norm_gain.reshape(1, features), kv_weight)


def finish_body(features, marks_ref, *refs):
    pieces, (fresh_ref, payload_ref) = refs[:-2], refs[-2:]
    slots, _, rows, width = fresh_ref.shape
    count = slots * rows
    total = pieces[0][...].astype(jnp.float32)
    for piece in pieces[1:]:
        total += piece[...].astype(jnp.float32)
    lanes = round_up(count, 128)
    squares = total[count : count + 1, :lanes] + total[count + 1 : count + 2, :lanes]
    inverse = lax.rsqrt(squares / features + EPS)
    inverse = jnp.transpose(jnp.broadcast_to(inverse, (lanes, lanes)))[:count, :width]
    for half in range(2):
        values = total[:count, half * width : (half + 1) * width] * inverse
        for slot in range(slots):
            mine = values[slot * rows : (slot + 1) * rows]
            fresh_ref[slot, half] = mine.astype(jnp.bfloat16)
            marked = jnp.concatenate([mine, marks_ref[slot]], 0)
            payload_ref[slot, half] = marked.astype(jnp.bfloat16)


def finish(pieces, marks, slots, rows, width, features):
    return pl.pallas_call(
        functools.partial(finish_body, features),
        out_shape=[
            jax.ShapeDtypeStruct((slots, 2, rows, width), jnp.bfloat16),
            jax.ShapeDtypeStruct((slots, 2, rows + marks.shape[1], width), jnp.bfloat16),
        ],
        cost_estimate=pl.CostEstimate(flops=1000, bytes_accessed=1000, transcendentals=0),
        name="finish",
    )(marks, *pieces)


def attend_body(sizes, locate, slot_ref, length_ref, place_ref, seq_ref, *refs):
    cached_count, fresh_count, rows, span, scale = sizes
    cached, refs = refs[:cached_count], refs[cached_count:]
    fresh, refs = refs[:fresh_count], refs[fresh_count:]
    (query_ref, query_at_ref, query_cos_ref, query_sin_ref, cos_ref, sin_ref, base_cos_ref) = refs[:7]
    base_sin_ref, out_ref = refs[7:9]
    cached_buf, fresh_buf, turned, limit, top, mass, total, sems = refs[9:]
    slots, _, columns = out_ref.shape
    width = cached_buf.shape[-1]
    group = columns // width
    stretches = slot_ref.shape[0]
    factor = scale * math.log2(math.e)
    last = functools.reduce(jnp.maximum, [place_ref[s] for s in range(slots)])

    def copies(position, act):
        slot = slot_ref[position]
        for which, refs, buf in ((0, cached, cached_buf), (1, fresh, fresh_buf)):
            for wanted, piece, index in locate(slot, seq_ref[0], slots, which):

                @pl.when(wanted)
                def _(piece=piece, index=index, refs=refs, buf=buf, which=which):
                    act(
                        pltpu.make_async_copy(
                            refs[piece].at[index], buf.at[position], sems.at[position, which]
                        )
                    )

    def start(position, carry):
        copies(position, lambda copy: copy.start())
        return carry

    lax.fori_loop(0, last + 1, start, 0)

    for slot in range(slots):

        @pl.when(place_ref[slot] >= 0)
        def _(slot=slot):
            cosine, sine = query_cos_ref[slot], query_sin_ref[slot]
            for head in range(group):
                values = query_ref[slot, :, head * width : (head + 1) * width].astype(jnp.float32)
                turned[slot, head * rows : (head + 1) * rows] = turn(values, cosine, sine)
                limit[slot, head * rows : (head + 1) * rows] = query_at_ref[slot]

        @pl.when(place_ref[slot] < 0)
        def _(slot=slot):
            out_ref[slot] = jnp.zeros_like(out_ref[slot])

    flip = jnp.where(lax.broadcasted_iota(jnp.int32, (1, width), 1) < width // 2, -1.0, 1.0)

    def stretch(position, carry):
        copies(position, lambda copy: copy.wait())
        marks = fresh_buf[position, 0, rows - rows % 16 :].astype(jnp.float32)[rows % 16 : rows % 16 + 1]
        token = lax.broadcasted_iota(jnp.int32, (span, width), 0).astype(jnp.float32)
        chosen = jnp.where(token == marks, 1.0, 0.0).astype(jnp.bfloat16)[:, : fresh_buf.shape[2]]
        source = jnp.concatenate(
            [fresh_buf[position, 0], fresh_buf[position, 1], jnp.ones_like(fresh_buf[position, 0])], 1
        )
        placed = jnp.dot(chosen, source, preferred_element_type=jnp.float32)
        replaced = placed[:, 2 * width :] > 0.5
        keys = jnp.where(replaced, placed[:, :width], cached_buf[position, 0].astype(jnp.float32))
        values = jnp.where(
            replaced, placed[:, width : 2 * width], cached_buf[position, 1].astype(jnp.float32)
        ).astype(jnp.bfloat16)
        base_cos, base_sin = base_cos_ref[pl.ds(position, 1)], base_sin_ref[pl.ds(position, 1)]
        cosine = cos_ref[...] * base_cos - sin_ref[...] * base_sin
        sine = (sin_ref[...] * base_cos + cos_ref[...] * base_sin) * flip
        keys = turn(keys, cosine, sine).astype(jnp.bfloat16)
        length = length_ref[position]
        index = lax.broadcasted_iota(jnp.int32, (1, span), 1)

        for slot in range(slots):

            @pl.when(place_ref[slot] >= position)
            def _(slot=slot):
                scores = lax.dot_general(
                    turned[slot].astype(jnp.bfloat16),
                    keys,
                    (((1,), (1,)), ((), ())),
                    preferred_element_type=jnp.float32,
                )
                bound = jnp.minimum(limit[slot] - position * span, length - 1)
                bound = jnp.concatenate([bound] * (span // width), 1)
                scores = jnp.where(index <= bound, scores, FAR)
                here = jnp.max(scores, 1, keepdims=True)

                @pl.when(position == 0)
                def _():
                    weight = jnp.exp2((scores - here) * factor)
                    top[slot] = jnp.broadcast_to(here, top.shape[1:])
                    mass[slot] = jnp.broadcast_to(jnp.sum(weight, 1, keepdims=True), mass.shape[1:])
                    total[slot] = jnp.dot(
                        weight.astype(jnp.bfloat16), values, preferred_element_type=jnp.float32
                    )

                @pl.when(position > 0)
                def _():
                    before = top[slot]
                    after = jnp.maximum(before, here)
                    fade = jnp.exp2((before - after) * factor)
                    weight = jnp.exp2((scores - after[:, :1]) * factor)
                    top[slot] = after
                    mass[slot] = mass[slot] * fade + jnp.sum(weight, 1, keepdims=True)
                    total[slot] = total[slot] * fade + jnp.dot(
                        weight.astype(jnp.bfloat16), values, preferred_element_type=jnp.float32
                    )

        return carry

    lax.fori_loop(0, last + 1, stretch, 0)

    for slot in range(slots):

        @pl.when(place_ref[slot] >= 0)
        def _(slot=slot):
            result = total[slot] / mass[slot]
            for head in range(group):
                out_ref[slot, :, head * width : (head + 1) * width] = result[
                    head * rows : (head + 1) * rows
                ].astype(jnp.bfloat16)


def attend(locate, cached, fresh, tables, queries, stretch_slot, stretch_lengths, my_pos, seq):
    slots, rows, columns = queries.shape
    span, width = cached[0].shape[-2:]
    lines = rows * (columns // width)
    stretches = stretch_slot.shape[0]
    padded = fresh[0].shape[-2]
    sizes = (len(cached), len(fresh), rows, span, width ** (-0.5))
    small = [pl.BlockSpec(memory_space=SMEM)] * 4
    far = [pl.BlockSpec(memory_space=pl.ANY)] * (len(cached) + len(fresh))
    near = [pl.BlockSpec(memory_space=VMEM)] * (1 + len(tables))
    return pl.pallas_call(
        functools.partial(attend_body, sizes, locate),
        out_shape=jax.ShapeDtypeStruct(queries.shape, jnp.bfloat16),
        in_specs=small + far + near,
        out_specs=pl.BlockSpec(memory_space=VMEM),
        scratch_shapes=[
            pltpu.VMEM((stretches, 2, span, width), jnp.bfloat16),
            pltpu.VMEM((stretches, 2, padded, width), jnp.bfloat16),
            pltpu.VMEM((slots, lines, width), jnp.float32),
            pltpu.VMEM((slots, lines, width), jnp.int32),
            pltpu.VMEM((slots, lines, width), jnp.float32),
            pltpu.VMEM((slots, lines, width), jnp.float32),
            pltpu.VMEM((slots, lines, width), jnp.float32),
            pltpu.SemaphoreType.DMA((stretches, 2)),
        ],
        cost_estimate=pl.CostEstimate(flops=1000, bytes_accessed=1000, transcendentals=0),
        compiler_params=pltpu.CompilerParams(vmem_limit_bytes=48 << 20),
        name="attend",
    )(stretch_slot, stretch_lengths, my_pos, seq, *cached, *fresh, queries, *tables)


def locate_gathered(slot, seq, slots, which):
    return [(slot >= 0, 0, slot)]


def locate_exchanged(slot, seq, slots, which):
    away = (slot // slots) ^ seq
    index = slot % slots
    if which == 1:
        return [(away == k, k, index) for k in range(4)]
    return [
        (away == 0, 0, index),
        (away == 1, 1, index),
        ((away == 2) & (index == 0), 2, 0),
        ((away == 3) & (index == 1), 3, 0),
        ((away == 2) & (index == 1), 4, 0),
        ((away == 3) & (index == 0), 5, 0),
    ]


def local(
    pool_kv, hidden_rows, norm_gain, kv_weight, queries, stretch_slot, stretch_lengths, recompute_rows
):
    slots, _, span, width = pool_kv.shape
    rows = recompute_rows.shape[1]
    stretches = stretch_slot.shape[0]
    seq_count = lax.axis_size("seq")
    seq = lax.axis_index("seq")
    parts = lax.axis_size(FEATURES)
    me = lax.axis_index(FEATURES)
    features = hidden_rows.shape[2] * parts
    exchanged = seq_count == 4 and slots == 2

    def along_seq(value, distance):
        return lax.ppermute(value, "seq", [(z, z ^ distance) for z in range(seq_count)])

    if exchanged:
        across = along_seq(pool_kv[0:1], 2)
        astray = along_seq(pool_kv[1:2], 3)
        beside = along_seq(pool_kv, 1)

    pieces = project(me.reshape(1).astype(jnp.int32), hidden_rows, norm_gain, kv_weight, parts)
    sums = [pieces[0]]
    for distance in range(parts - 1, 0, -1):
        sums.append(
            lax.ppermute(pieces[distance], FEATURES, [(i, i ^ distance) for i in range(parts)])
        )
    marks = jnp.pad(recompute_rows.astype(jnp.float32), ((0, 0), (0, width - rows)), constant_values=-1.0)
    marks = jnp.broadcast_to(marks[:, None], (slots, 8, width))
    fresh_kv, payload = finish(sums, marks, slots, rows, width, features)

    mine = seq * slots + jnp.arange(slots, dtype=jnp.int32)
    hits = stretch_slot[:, None] == mine[None]
    order = jnp.arange(stretches, dtype=jnp.int32)[:, None]
    my_pos = jnp.max(jnp.where(hits, order, -1), 0)
    query_at = my_pos[:, None] * span + recompute_rows
    inverse = THETA ** (-2.0 * np.arange(width // 2) / width)
    inverse = np.concatenate([inverse, inverse]).astype(np.float32)
    angle = query_at.astype(jnp.float32)[..., None] * inverse
    flip = np.where(np.arange(width) < width // 2, -1.0, 1.0).astype(np.float32)
    tables = (
        jnp.broadcast_to(query_at[..., None], (slots, rows, width)),
        jnp.cos(angle),
        jnp.sin(angle) * flip,
        *rope_tables(np.arange(span), width),
        *rope_tables(np.arange(stretches) * span, width),
    )

    if exchanged:
        cached = [pool_kv, beside, across, astray, along_seq(astray, 1), along_seq(across, 1)]
        fresh = [payload, along_seq(payload, 1), along_seq(payload, 2), along_seq(payload, 3)]
        locate = locate_exchanged
    else:
        cached = [lax.all_gather(pool_kv, "seq", axis=0, tiled=True)]
        fresh = [lax.all_gather(payload, "seq", axis=0, tiled=True)]
        locate = locate_gathered
    attended = attend(
        locate, cached, fresh, tables, queries, stretch_slot, stretch_lengths, my_pos, seq.reshape(1)
    )
    return fresh_kv, attended


def solution(mesh):
    in_specs = (
        P(("groups", "seq"), None, None, FEATURES),
        P(("groups", "seq"), None, FEATURES),
        P(FEATURES),
        P(FEATURES, None),
        P(("groups", "seq"), None, FEATURES),
        P("groups"),
        P("groups"),
        P(("groups", "seq"), None),
    )
    out_specs = (
        P(("groups", "seq"), None, None, FEATURES),
        P(("groups", "seq"), None, FEATURES),
    )
    return jax.shard_map(local, mesh=mesh, in_specs=in_specs, out_specs=out_specs, check_vma=False)
```

```python
import functools
import math

import jax
import jax.numpy as jnp
import numpy as np
from jax import lax
from jax.experimental import pallas as pl
from jax.experimental.pallas import tpu as pltpu
from jax.sharding import PartitionSpec as P

THETA = 500000.0
EPS = 1e-05
FAR = -1e30
FEATURES = ("tp", "kvh")
VMEM = pltpu.MemorySpace.VMEM
SMEM = pltpu.MemorySpace.SMEM
PROJECT_VMEM = 61 << 20


def round_up(value, step):
    return -(-value // step) * step


def rope_tables(positions, width):
    inverse = THETA ** (-2.0 * np.arange(width // 2) / width)
    angle = np.asarray(positions, np.float64)[:, None] * np.concatenate([inverse, inverse])[None]
    return np.cos(angle).astype(np.float32), np.sin(angle).astype(np.float32)


def turn(values, cosine, sine):
    return values * cosine + pltpu.roll(values, values.shape[-1] // 2, 1) * sine


def project_body(me_ref, hidden_ref, gain_ref, weight_ref, *refs):
    pieces, (held, gain, weights, whole, sems) = refs[:-5], refs[-5:]
    chunks, depth, width = weights.shape
    slots, rows, features = held.shape
    count = slots * rows
    height, columns = pieces[0].shape
    spare = height - count

    def chunk(k):
        part = weight_ref.at[pl.ds(k * depth, depth)]
        return pltpu.make_async_copy(part, weights.at[k], sems.at[2 + k])

    arrive = pltpu.make_async_copy(hidden_ref, held, sems.at[0])
    follow = pltpu.make_async_copy(gain_ref, gain, sems.at[1])
    arrive.start()
    follow.start()
    for k in range(chunks):
        chunk(k).start()
    arrive.wait()
    follow.wait()
    hidden = held[...].astype(jnp.float32).reshape(count, features)
    scaled = (hidden * gain[...].astype(jnp.float32).reshape(1, features)).astype(jnp.bfloat16)
    square = hidden * hidden
    fill = jnp.zeros((round_up(count, 128) - count, features), jnp.float32)
    square = jnp.concatenate([square, fill], 0)
    high = square.astype(jnp.bfloat16)
    low = (square - high.astype(jnp.float32)).astype(jnp.bfloat16)
    ones = jnp.ones((spare, features), jnp.bfloat16)
    along = (((1,), (1,)), ((), ()))
    total = lax.dot_general(ones, high, along, preferred_element_type=jnp.float32)
    total += lax.dot_general(ones, low, along, preferred_element_type=jnp.float32)
    coarse = total.astype(jnp.bfloat16).astype(jnp.float32)
    row = lax.broadcasted_iota(jnp.int32, total.shape, 0)
    both = jnp.where(row == 0, coarse, jnp.where(row == 1, total - coarse, 0.0))
    rest = jnp.zeros((spare, columns - total.shape[1]), jnp.float32)
    tail = jnp.concatenate([both, rest], 1).astype(jnp.bfloat16)
    product = jnp.zeros((count, width), jnp.float32)
    for k in range(chunks):
        chunk(k).wait()
        part = scaled[:, k * depth : (k + 1) * depth]
        product += jnp.dot(part, weights[k], preferred_element_type=jnp.float32)
    whole[...] = product
    for k, piece in enumerate(pieces):
        at = pl.multiple_of((me_ref[0] ^ k) * columns, columns)
        piece[:count] = whole[:, pl.ds(at, columns)].astype(jnp.bfloat16)
        piece[count:] = tail


def project(me, hidden_rows, norm_gain, kv_weight, parts):
    slots, rows, features = hidden_rows.shape
    columns = kv_weight.shape[1] // parts
    chunks = 4
    shape = (slots * rows + 16, columns)
    return pl.pallas_call(
        project_body,
        out_shape=[jax.ShapeDtypeStruct(shape, jnp.bfloat16)] * parts,
        in_specs=[pl.BlockSpec(memory_space=SMEM)] + [pl.BlockSpec(memory_space=pltpu.HBM)] * 3,
        out_specs=[pl.BlockSpec(memory_space=VMEM)] * parts,
        scratch_shapes=[
            pltpu.VMEM(hidden_rows.shape, jnp.bfloat16),
            pltpu.VMEM(norm_gain.shape, jnp.bfloat16),
            pltpu.VMEM((chunks, features // chunks, kv_weight.shape[1]), jnp.bfloat16),
            pltpu.VMEM((slots * rows, kv_weight.shape[1]), jnp.float32),
            pltpu.SemaphoreType.DMA((2 + chunks,)),
        ],
        cost_estimate=pl.CostEstimate(flops=1000, bytes_accessed=1000, transcendentals=0),
        compiler_params=pltpu.CompilerParams(vmem_limit_bytes=PROJECT_VMEM),
        name="project",
    )(me, hidden_rows, norm_gain, kv_weight)


def finish_body(features, marks_ref, *refs):
    pieces, (fresh_ref, payload_ref) = refs[:-2], refs[-2:]
    slots, _, rows, width = fresh_ref.shape
    count = slots * rows
    total = pieces[0][...].astype(jnp.float32)
    for piece in pieces[1:]:
        total += piece[...].astype(jnp.float32)
    lanes = round_up(count, 128)
    squares = total[count : count + 1, :lanes] + total[count + 1 : count + 2, :lanes]
    inverse = lax.rsqrt(squares / features + EPS)
    inverse = jnp.transpose(jnp.broadcast_to(inverse, (lanes, lanes)))[:count, :width]
    for half in range(2):
        values = total[:count, half * width : (half + 1) * width] * inverse
        for slot in range(slots):
            mine = values[slot * rows : (slot + 1) * rows]
            fresh_ref[slot, half] = mine.astype(jnp.bfloat16)
            marks = jnp.broadcast_to(marks_ref[slot : slot + 1], (payload_ref.shape[2] - rows, width))
            marked = jnp.concatenate([mine, marks], 0)
            payload_ref[slot, half] = marked.astype(jnp.bfloat16)


def finish(pieces, marks, slots, rows, width, features):
    return pl.pallas_call(
        functools.partial(finish_body, features),
        out_shape=[
            jax.ShapeDtypeStruct((slots, 2, rows, width), jnp.bfloat16),
            jax.ShapeDtypeStruct((slots, 2, round_up(rows + 1, 16), width), jnp.bfloat16),
        ],
        cost_estimate=pl.CostEstimate(flops=1000, bytes_accessed=1000, transcendentals=0),
        compiler_params=pltpu.CompilerParams(vmem_limit_bytes=8 << 20),
        name="finish",
    )(marks, *pieces)


def tie_body(*refs):
    pass


def tie(value, others):
    return pl.pallas_call(
        tie_body,
        out_shape=jax.ShapeDtypeStruct(value.shape, value.dtype),
        in_specs=[pl.BlockSpec(memory_space=pl.ANY)] * (1 + len(others)),
        out_specs=pl.BlockSpec(memory_space=pl.ANY),
        input_output_aliases={0: 0},
        cost_estimate=pl.CostEstimate(flops=1000, bytes_accessed=1000, transcendentals=0),
        compiler_params=pltpu.CompilerParams(vmem_limit_bytes=1 << 20),
        name="tie",
    )(value, *others)


def ready(cached_buf, fresh_buf, position, rows, tables):
    cos_ref, sin_ref, base_cos_ref, base_sin_ref = tables
    span, width = cached_buf.shape[-2:]
    start = rows - rows % 16
    marks = fresh_buf[position, 0, start:].astype(jnp.float32)[rows - start : rows - start + 1]
    token = lax.broadcasted_iota(jnp.int32, (span, width), 0).astype(jnp.float32)
    chosen = jnp.where(token == marks, 1.0, 0.0).astype(jnp.bfloat16)[:, : fresh_buf.shape[-2]]
    keys, values = fresh_buf[position, 0], fresh_buf[position, 1]
    source = jnp.concatenate([keys, values, jnp.ones_like(keys)], 1)
    placed = jnp.dot(chosen, source, preferred_element_type=jnp.float32)
    replaced = placed[:, 2 * width :] > 0.5
    old_keys, old_values = cached_buf[position, 0], cached_buf[position, 1]
    keys = jnp.where(replaced, placed[:, :width], old_keys.astype(jnp.float32))
    values = jnp.where(replaced, placed[:, width : 2 * width], old_values.astype(jnp.float32))
    base_cos, base_sin = base_cos_ref[pl.ds(position, 1)], base_sin_ref[pl.ds(position, 1)]
    flip = jnp.where(lax.broadcasted_iota(jnp.int32, (1, width), 1) < width // 2, -1.0, 1.0)
    cosine = cos_ref[...] * base_cos - sin_ref[...] * base_sin
    sine = (sin_ref[...] * base_cos + cos_ref[...] * base_sin) * flip
    return turn(keys, cosine, sine).astype(jnp.bfloat16), values.astype(jnp.bfloat16)


def fetch(act, places, cached, fresh, cached_buf, fresh_buf, sems, position):
    for wanted, piece, index in places:

        @pl.when(wanted)
        def _(piece=piece, index=index):
            for which, refs, buf in ((0, cached, cached_buf), (1, fresh, fresh_buf)):
                act(
                    pltpu.make_async_copy(
                        refs[piece].at[index], buf.at[position], sems.at[position, which]
                    )
                )


def score(query, keys):
    along = (((1,), (1,)), ((), ()))
    return lax.dot_general(query, keys, along, preferred_element_type=jnp.float32)


def absorb(first, state, scores, values, factor):
    top, mass, total = state
    before = jnp.where(first, FAR, top[...])
    after = jnp.maximum(before, jnp.max(scores, 1, keepdims=True))
    fade = jnp.where(first, 0.0, jnp.exp2((before - after) * factor))
    weight = jnp.exp2((scores - after[:, :1]) * factor)
    top[...] = after
    mass[...] = jnp.where(first, 0.0, mass[...]) * fade + jnp.sum(weight, 1, keepdims=True)
    total[...] = jnp.where(first, 0.0, total[...]) * fade + jnp.dot(
        weight.astype(jnp.bfloat16), values, preferred_element_type=jnp.float32
    )


def early_body(pieces, locate, rows, factor, slot_ref, length_ref, place_ref, seq_ref, *refs):
    cached, fresh, refs = refs[:pieces], refs[pieces : 2 * pieces], refs[2 * pieces :]
    query_ref, query_at_ref, query_cos_ref, query_sin_ref, *tables = refs[:8]
    turned, top, mass, total, cached_buf, fresh_buf, keys_buf, values_buf, sems = refs[8:]
    slots, _, columns = query_ref.shape
    span, width = cached_buf.shape[-2:]
    group = columns // width
    stretches = slot_ref.shape[0]
    last = functools.reduce(jnp.maximum, [place_ref[s] for s in range(slots)])

    def there(position):
        places = locate(slot_ref[position], seq_ref[0], slots)
        return functools.reduce(jnp.logical_or, [place[0] for place in places])

    def copies(position, act):
        places = locate(slot_ref[position], seq_ref[0], slots)
        fetch(act, places, cached, fresh, cached_buf, fresh_buf, sems, position)

    def start(position, carry):
        copies(position, lambda copy: copy.start())

        @pl.when(jnp.logical_not(there(position)))
        def _():
            cached_buf[position] = jnp.zeros_like(cached_buf[position])
            fresh_buf[position] = jnp.zeros_like(fresh_buf[position])

        return carry

    lax.fori_loop(0, last + 1, start, 0)

    def prepare(slot, carry):
        @pl.when(place_ref[slot] >= 0)
        def _():
            cosine, sine = query_cos_ref[slot], query_sin_ref[slot]
            heads = [
                turn(query_ref[slot, :, h * width : (h + 1) * width].astype(jnp.float32), cosine, sine)
                for h in range(group)
            ]
            turned[slot] = jnp.concatenate(heads, 0).astype(jnp.bfloat16)

        return carry

    lax.fori_loop(0, slots, prepare, 0)
    index = lax.broadcasted_iota(jnp.int32, (rows, span), 1)

    def wall(slot, position):
        limit = query_at_ref[slot] - position * span
        limit = jnp.concatenate([limit] * (span // width), 1)
        end = jnp.where(there(position), length_ref[position] - 1, -1)
        return jnp.where(index <= jnp.minimum(limit, end), 0.0, FAR)

    if stretches <= 4:
        for count in range(1, stretches + 1):

            @pl.when(last == count - 1)
            def _(count=count):
                for position in range(count):
                    copies(position, lambda copy: copy.wait())
                for position in range(count):
                    here = slice(position * span, (position + 1) * span)
                    keys_buf[here], values_buf[here] = ready(
                        cached_buf, fresh_buf, position, rows, tables
                    )

        def one(slot, carry):
            for count in range(1, stretches + 1):

                @pl.when(place_ref[slot] == count - 1)
                def _(count=count):
                    walls = [wall(slot, position) for position in range(count)]
                    walls = jnp.concatenate([jnp.concatenate(walls, 1)] * group, 0)
                    scores = score(turned[slot], keys_buf[: count * span]) + walls
                    highest = jnp.max(scores, 1, keepdims=True)
                    weight = jnp.exp2((scores - highest) * factor)
                    shape = top.shape[1:]
                    top[slot] = jnp.broadcast_to(highest, shape)
                    mass[slot] = jnp.broadcast_to(jnp.sum(weight, 1, keepdims=True), shape)
                    total[slot] = jnp.dot(
                        weight.astype(jnp.bfloat16),
                        values_buf[: count * span],
                        preferred_element_type=jnp.float32,
                    )

            return carry

        lax.fori_loop(0, slots, one, 0)
        return

    def stretch(position, carry):
        copies(position, lambda copy: copy.wait())
        keys_buf[:span], values_buf[:span] = ready(cached_buf, fresh_buf, position, rows, tables)

        def one(slot, carry):
            @pl.when(place_ref[slot] >= position)
            def _():
                walls = jnp.concatenate([wall(slot, position)] * group, 0)
                scores = score(turned[slot], keys_buf[:span]) + walls
                state = [ref.at[slot] for ref in (top, mass, total)]
                absorb(position == 0, state, scores, values_buf[:span], factor)

            return carry

        return lax.fori_loop(0, slots, one, carry)

    lax.fori_loop(0, last + 1, stretch, 0)


def late_body(pieces, locate, rows, factor, slot_ref, length_ref, place_ref, seq_ref, *refs):
    cached, fresh, refs = refs[:pieces], refs[pieces : 2 * pieces], refs[2 * pieces :]
    tables, (turned, early_top, early_mass, early_total, out_ref) = refs[:4], refs[4:9]
    top, mass, total, cached_buf, fresh_buf, sems = refs[9:]
    slots, _, columns = out_ref.shape
    span, width = cached_buf.shape[-2:]
    group = columns // width
    stretches = slot_ref.shape[0]
    last = functools.reduce(jnp.maximum, [place_ref[s] for s in range(slots)])

    def copies(position, act):
        places = locate(slot_ref[position], seq_ref[0], slots)
        places = [(wanted & (position < last), piece, index) for wanted, piece, index in places]
        fetch(act, places, cached, fresh, cached_buf, fresh_buf, sems, position)
        return functools.reduce(jnp.logical_or, [place[0] for place in places])

    if pieces:
        for position in range(stretches):
            copies(position, lambda copy: copy.start())
    for slot in range(slots):

        @pl.when(place_ref[slot] >= 0)
        def _(slot=slot):
            top[slot], mass[slot], total[slot] = early_top[slot], early_mass[slot], early_total[slot]

    def stretch(position, carry):
        @pl.when(copies(position, lambda copy: copy.wait()))
        def _():
            keys, values = ready(cached_buf, fresh_buf, position, rows, tables)
            index = lax.broadcasted_iota(jnp.int32, (1, span), 1)
            walls = jnp.where(index < length_ref[position], 0.0, FAR)
            for slot in range(slots):

                @pl.when(place_ref[slot] > position)
                def _(slot=slot):
                    scores = score(turned[slot], keys) + walls
                    absorb(False, [ref.at[slot] for ref in (top, mass, total)], scores, values, factor)

        return carry

    if pieces:
        lax.fori_loop(0, stretches, stretch, 0)
    for slot in range(slots):

        @pl.when(place_ref[slot] >= 0)
        def _(slot=slot):
            result = total[slot] / mass[slot]
            for head in range(group):
                mine = result[head * rows : (head + 1) * rows]
                out_ref[slot, :, head * width : (head + 1) * width] = mine.astype(jnp.bfloat16)

        @pl.when(place_ref[slot] < 0)
        def _(slot=slot):
            out_ref[slot] = jnp.zeros_like(out_ref[slot])


def attend(body, locate, lists, cached, fresh, near, out_shape, scratch, sizes, cost):
    rows, stretches, padded, span, width = sizes
    factor = width ** (-0.5) * math.log2(math.e)
    specs = [pl.BlockSpec(memory_space=SMEM)] * len(lists)
    specs += [pl.BlockSpec(memory_space=pl.ANY)] * (len(cached) + len(fresh))
    specs += [pl.BlockSpec(memory_space=VMEM)] * len(near)
    return pl.pallas_call(
        functools.partial(body, len(cached), locate, rows, factor),
        out_shape=out_shape,
        in_specs=specs,
        out_specs=jax.tree.map(lambda _: pl.BlockSpec(memory_space=VMEM), out_shape),
        scratch_shapes=[
            *scratch[0],
            pltpu.VMEM((stretches, 2, span, width), jnp.bfloat16),
            pltpu.VMEM((stretches, 2, padded, width), jnp.bfloat16),
            *scratch[1],
            pltpu.SemaphoreType.DMA((stretches, 2)),
        ],
        cost_estimate=pl.CostEstimate(flops=cost, bytes_accessed=1000, transcendentals=0),
        compiler_params=pltpu.CompilerParams(vmem_limit_bytes=32 << 20),
        name=body.__name__,
    )(*lists, *cached, *fresh, *near)


def locate_all(slot, seq, slots):
    return [(slot >= 0, 0, slot)]


def locate_early(slot, seq, slots):
    away = (slot // slots) ^ seq
    return [(away == k, k, slot % slots) for k in range(3)]


def locate_late(slot, seq, slots):
    return [((slot // slots) ^ seq == 3, 0, slot % slots)]


def local(
    pool_kv, hidden_rows, norm_gain, kv_weight, queries, stretch_slot, stretch_lengths, recompute_rows
):
    slots, _, span, width = pool_kv.shape
    rows = recompute_rows.shape[1]
    stretches = stretch_slot.shape[0]
    seq_count = lax.axis_size("seq")
    seq = lax.axis_index("seq")
    parts = lax.axis_size(FEATURES)
    me = lax.axis_index(FEATURES)
    features = hidden_rows.shape[2] * parts
    exchanged = seq_count == 4 and slots == 2
    padded = round_up(rows + 1, 16)

    def along_seq(value, distance):
        return lax.ppermute(value, "seq", [(z, z ^ distance) for z in range(seq_count)])

    if exchanged:
        across = along_seq(pool_kv, 2)
        beside = along_seq(pool_kv, 1)

    marks = jnp.pad(recompute_rows.astype(jnp.float32), ((0, 0), (0, width - rows)), constant_values=-1.0)

    pieces = project(me.reshape(1).astype(jnp.int32), hidden_rows, norm_gain, kv_weight, parts)
    sums = [pieces[0]]
    for distance in range(parts - 1, 0, -1):
        swap = [(i, i ^ distance) for i in range(parts)]
        sums.append(lax.ppermute(pieces[distance], FEATURES, swap))
    fresh_kv, payload = finish(sums, marks, slots, rows, width, features)

    mine = seq * slots + jnp.arange(slots, dtype=jnp.int32)
    hits = stretch_slot[:, None] == mine[None]
    order = jnp.arange(stretches, dtype=jnp.int32)[:, None]
    my_pos = jnp.max(jnp.where(hits, order, -1), 0)
    query_at = my_pos[:, None] * span + recompute_rows
    inverse = THETA ** (-2.0 * np.arange(width // 2) / width)
    inverse = np.concatenate([inverse, inverse]).astype(np.float32)
    angle = query_at.astype(jnp.float32)[..., None] * inverse
    flip = np.where(np.arange(width) < width // 2, -1.0, 1.0).astype(np.float32)
    query_tables = (
        jnp.broadcast_to(query_at[..., None], (slots, rows, width)),
        jnp.cos(angle),
        jnp.sin(angle) * flip,
    )
    tables = (*rope_tables(np.arange(span), width), *rope_tables(np.arange(stretches) * span, width))

    if exchanged:
        across = tie(across, [beside, payload])
        beyond = along_seq(across, 1)
        payloads = [payload, *[along_seq(payload, k) for k in (1, 2, 3)]]
        early, late = ([pool_kv, beside, across], payloads[:3]), ([beyond], payloads[3:])
        locate = locate_early
    else:
        early = [[lax.all_gather(array, "seq", axis=0, tiled=True)] for array in (pool_kv, payload)]
        late = ([], [])
        locate = locate_all

    lists = (stretch_slot, stretch_lengths, my_pos, seq.reshape(1))
    lines = rows * (queries.shape[2] // width)
    sizes = (rows, stretches, padded, span, width)
    state = jax.ShapeDtypeStruct((slots, lines, width), jnp.float32)
    held = pltpu.VMEM((slots, lines, width), jnp.float32)
    stage = pltpu.VMEM(((stretches if stretches <= 4 else 1) * span, width), jnp.bfloat16)
    passed = attend(
        early_body,
        locate,
        lists,
        *early,
        (queries, *query_tables, *tables),
        [jax.ShapeDtypeStruct((slots, lines, width), jnp.bfloat16), state, state, state],
        ([], [stage, stage]),
        sizes,
        10**10,
    )
    attended = attend(
        late_body,
        locate_late,
        lists,
        *late,
        (*tables, *passed),
        jax.ShapeDtypeStruct(queries.shape, jnp.bfloat16),
        ([held, held, held], []),
        sizes,
        1000,
    )
    return fresh_kv, attended


def solution(mesh):
    in_specs = (
        P(("groups", "seq"), None, None, FEATURES),
        P(("groups", "seq"), None, FEATURES),
        P(FEATURES),
        P(FEATURES, None),
        P(("groups", "seq"), None, FEATURES),
        P("groups"),
        P("groups"),
        P(("groups", "seq"), None),
    )
    out_specs = (
        P(("groups", "seq"), None, None, FEATURES),
        P(("groups", "seq"), None, FEATURES),
    )
    return jax.shard_map(local, mesh=mesh, in_specs=in_specs, out_specs=out_specs, check_vma=False)
```

```python
import functools
import math

import jax
import jax.numpy as jnp
import numpy as np
from jax import lax
from jax.experimental import pallas as pl
from jax.experimental.pallas import tpu as pltpu
from jax.sharding import PartitionSpec as P

THETA = 500000.0
EPS = 1e-05
FAR = -1e30
FEATURES = ("tp", "kvh")
VMEM = pltpu.MemorySpace.VMEM
SMEM = pltpu.MemorySpace.SMEM
PROJECT_VMEM = 61 << 20
EARLY_COST = 3*10**9


def round_up(value, step):
    return -(-value // step) * step


def rope_tables(positions, width):
    inverse = THETA ** (-2.0 * np.arange(width // 2) / width)
    angle = np.asarray(positions, np.float64)[:, None] * np.concatenate([inverse, inverse])[None]
    return np.cos(angle).astype(np.float32), np.sin(angle).astype(np.float32)


def turn(values, cosine, sine):
    return values * cosine + pltpu.roll(values, values.shape[-1] // 2, 1) * sine


def place_of(slot, slot_ref):
    place = jnp.int32(-1)
    for position in range(slot_ref.shape[0]):
        place = jnp.where(slot_ref[position] == slot, jnp.int32(position), place)
    return place


def outer(seq):
    return jnp.where((seq == 0) | (seq == 3), 1, 0)


def far_slots(seq, slot_ref):
    last = jnp.maximum(*[place_of(2 * seq + j, slot_ref) for j in range(2)])
    slots = [2 * (seq ^ 3) + j for j in range(2)]
    slots = [jnp.where(place_of(slot, slot_ref) < last, slot, -1) for slot in slots]
    slots = [jnp.where(place_of(slot, slot_ref) < 0, -1, slot) for slot in slots]
    return [jnp.where(slots[0] >= 0, slots[0], slots[1]), jnp.where(slots[0] >= 0, slots[1], -1)]


def project_body(me_ref, hidden_ref, gain_ref, weight_ref, *refs):
    *pieces, held, gain, weights, whole, sems = refs
    chunks, depth, width = weights.shape
    slots, rows, features = held.shape
    count = slots * rows
    height, columns = pieces[0].shape
    spare = height - count

    def chunk(k):
        part = weight_ref.at[pl.ds(k * depth, depth)]
        return pltpu.make_async_copy(part, weights.at[k], sems.at[2 + k])

    arrive = pltpu.make_async_copy(hidden_ref, held, sems.at[0])
    follow = pltpu.make_async_copy(gain_ref, gain, sems.at[1])
    arrive.start()
    follow.start()
    for k in range(chunks):
        chunk(k).start()
    arrive.wait()
    follow.wait()
    hidden = held[...].astype(jnp.float32).reshape(count, features)
    scaled = (hidden * gain[...].astype(jnp.float32).reshape(1, features)).astype(jnp.bfloat16)
    square = hidden * hidden
    fill = jnp.zeros((round_up(count, 128) - count, features), jnp.float32)
    square = jnp.concatenate([square, fill], 0)
    high = square.astype(jnp.bfloat16)
    low = (square - high.astype(jnp.float32)).astype(jnp.bfloat16)
    ones = jnp.ones((spare, features), jnp.bfloat16)
    along = (((1,), (1,)), ((), ()))
    total = lax.dot_general(ones, high, along, preferred_element_type=jnp.float32)
    total += lax.dot_general(ones, low, along, preferred_element_type=jnp.float32)
    coarse = total.astype(jnp.bfloat16).astype(jnp.float32)
    row = lax.broadcasted_iota(jnp.int32, total.shape, 0)
    both = jnp.where(row == 0, coarse, jnp.where(row == 1, total - coarse, 0.0))
    rest = jnp.zeros((spare, columns - total.shape[1]), jnp.float32)
    tail = jnp.concatenate([both, rest], 1).astype(jnp.bfloat16)
    product = jnp.zeros((count, width), jnp.float32)
    for k in range(chunks):
        chunk(k).wait()
        part = scaled[:, k * depth : (k + 1) * depth]
        product += jnp.dot(part, weights[k], preferred_element_type=jnp.float32)
    whole[...] = product
    for k, piece in enumerate(pieces):
        at = pl.multiple_of((me_ref[0] ^ k) * columns, columns)
        piece[:count] = whole[:, pl.ds(at, columns)].astype(jnp.bfloat16)
        piece[count:] = tail


def project(me, hidden_rows, norm_gain, kv_weight, parts):
    slots, rows, features = hidden_rows.shape
    columns = kv_weight.shape[1] // parts
    chunks = 4
    shape = (slots * rows + 16, columns)
    return pl.pallas_call(
        project_body,
        out_shape=[jax.ShapeDtypeStruct(shape, jnp.bfloat16)] * parts,
        in_specs=[pl.BlockSpec(memory_space=SMEM)] + [pl.BlockSpec(memory_space=pltpu.HBM)] * 3,
        out_specs=[pl.BlockSpec(memory_space=VMEM)] * parts,
        scratch_shapes=[
            pltpu.VMEM(hidden_rows.shape, jnp.bfloat16),
            pltpu.VMEM(norm_gain.shape, jnp.bfloat16),
            pltpu.VMEM((chunks, features // chunks, kv_weight.shape[1]), jnp.bfloat16),
            pltpu.VMEM((slots * rows, kv_weight.shape[1]), jnp.float32),
            pltpu.SemaphoreType.DMA((2 + chunks,)),
        ],
        cost_estimate=pl.CostEstimate(flops=1000, bytes_accessed=1000, transcendentals=0),
        compiler_params=pltpu.CompilerParams(vmem_limit_bytes=PROJECT_VMEM),
        name="project",
    )(me, hidden_rows, norm_gain, kv_weight)


def finish_body(features, marks_ref, *refs):
    pieces, (fresh_ref, payload_ref) = refs[:-2], refs[-2:]
    slots, _, rows, width = fresh_ref.shape
    count = slots * rows
    total = pieces[0][...].astype(jnp.float32)
    for piece in pieces[1:]:
        total += piece[...].astype(jnp.float32)
    lanes = round_up(count, 128)
    squares = total[count : count + 1, :lanes] + total[count + 1 : count + 2, :lanes]
    inverse = lax.rsqrt(squares / features + EPS)
    inverse = jnp.transpose(jnp.broadcast_to(inverse, (lanes, lanes)))[:count, :width]
    for half in range(2):
        values = total[:count, half * width : (half + 1) * width] * inverse
        for slot in range(slots):
            mine = values[slot * rows : (slot + 1) * rows]
            fresh_ref[slot, half] = mine.astype(jnp.bfloat16)
            marks = jnp.broadcast_to(marks_ref[slot : slot + 1], (payload_ref.shape[2] - rows, width))
            marked = jnp.concatenate([mine, marks], 0)
            payload_ref[slot, half] = marked.astype(jnp.bfloat16)


def finish(pieces, marks, slots, rows, width, features):
    return pl.pallas_call(
        functools.partial(finish_body, features),
        out_shape=[
            jax.ShapeDtypeStruct((slots, 2, rows, width), jnp.bfloat16),
            jax.ShapeDtypeStruct((slots, 2, round_up(rows + 1, 16), width), jnp.bfloat16),
        ],
        cost_estimate=pl.CostEstimate(flops=1000, bytes_accessed=1000, transcendentals=0),
        compiler_params=pltpu.CompilerParams(vmem_limit_bytes=8 << 20),
        name="finish",
    )(marks, *pieces)


def assemble_body(seq_ref, one_ref, two_ref, ahead_ref, out_ref, sem):
    del ahead_ref
    at_end = outer(seq_ref[0])
    for wanted, ref in ((0, one_ref), (1, two_ref)):

        @pl.when(at_end == wanted)
        def _(ref=ref):
            copy = pltpu.make_async_copy(ref, out_ref, sem)
            copy.start()
            copy.wait()


def assemble(seq, one, two, ahead):
    far = pl.BlockSpec(memory_space=pl.ANY)
    return pl.pallas_call(
        assemble_body,
        out_shape=jax.ShapeDtypeStruct(one.shape, one.dtype),
        in_specs=[pl.BlockSpec(memory_space=SMEM), far, far, far],
        out_specs=pl.BlockSpec(memory_space=VMEM),
        scratch_shapes=[pltpu.SemaphoreType.DMA(())],
        cost_estimate=pl.CostEstimate(flops=1000, bytes_accessed=1000, transcendentals=0),
        compiler_params=pltpu.CompilerParams(vmem_limit_bytes=8 << 20),
        name="assemble",
    )(seq, one, two, ahead)


def hold_body(value_ref, *refs):
    refs[-1][...] = value_ref[...]


def hold(value, *ahead):
    near, far = pl.BlockSpec(memory_space=VMEM), pl.BlockSpec(memory_space=pl.ANY)
    return pl.pallas_call(
        hold_body,
        out_shape=jax.ShapeDtypeStruct(value.shape, value.dtype),
        in_specs=[near] + [far] * len(ahead),
        out_specs=near,
        cost_estimate=pl.CostEstimate(flops=1000, bytes_accessed=1000, transcendentals=0),
        compiler_params=pltpu.CompilerParams(vmem_limit_bytes=8 << 20),
        name="hold",
    )(value, *ahead)


def ready(cached, fresh, position, rows, tables):
    cos_ref, sin_ref, base_cos_ref, base_sin_ref = tables
    _, span, width = cached.shape
    start = rows - rows % 16
    marks = fresh[0, start:].astype(jnp.float32)[rows - start : rows - start + 1]
    token = lax.broadcasted_iota(jnp.int32, (span, width), 0).astype(jnp.float32)
    chosen = jnp.where(token == marks, 1.0, 0.0).astype(jnp.bfloat16)[:, : fresh.shape[-2]]
    keys, values = fresh[0], fresh[1]
    source = jnp.concatenate([keys, values, jnp.ones_like(keys)], 1)
    placed = jnp.dot(chosen, source, preferred_element_type=jnp.float32)
    replaced = placed[:, 2 * width :] > 0.5
    old_keys, old_values = cached[0], cached[1]
    keys = jnp.where(replaced, placed[:, :width], old_keys.astype(jnp.float32))
    values = jnp.where(replaced, placed[:, width : 2 * width], old_values.astype(jnp.float32))
    base_cos, base_sin = base_cos_ref[pl.ds(position, 1)], base_sin_ref[pl.ds(position, 1)]
    flip = jnp.where(lax.broadcasted_iota(jnp.int32, (1, width), 1) < width // 2, -1.0, 1.0)
    cosine = cos_ref[...] * base_cos - sin_ref[...] * base_sin
    sine = (sin_ref[...] * base_cos + cos_ref[...] * base_sin) * flip
    return turn(keys, cosine, sine).astype(jnp.bfloat16), values.astype(jnp.bfloat16)


def fetch(act, places, cached, fresh, cached_buf, fresh_buf, sems, position):
    for wanted, *sources in places:

        @pl.when(wanted)
        def _(sources=sources):
            for which, refs, buf in ((0, cached, cached_buf), (1, fresh, fresh_buf)):
                piece, index = sources[which]
                act(
                    pltpu.make_async_copy(
                        refs[piece].at[index], buf.at[position], sems.at[position, which]
                    )
                )


def score(query, keys):
    along = (((1,), (1,)), ((), ()))
    return lax.dot_general(query, keys, along, preferred_element_type=jnp.float32)


def absorb(first, state, scores, values, factor):
    top, mass, total = state
    before = jnp.where(first, FAR, top[...])
    after = jnp.maximum(before, jnp.max(scores, 1, keepdims=True))
    fade = jnp.where(first, 0.0, jnp.exp2((before - after) * factor))
    weight = jnp.exp2((scores - after[:, :1]) * factor)
    top[...] = after
    mass[...] = jnp.where(first, 0.0, mass[...]) * fade + jnp.sum(weight, 1, keepdims=True)
    total[...] = jnp.where(first, 0.0, total[...]) * fade + jnp.dot(
        weight.astype(jnp.bfloat16), values, preferred_element_type=jnp.float32
    )


def early_body(pieces, locate, rows, factor, slot_ref, length_ref, place_ref, seq_ref, *refs):
    cached, fresh, refs = refs[:pieces], refs[pieces : 2 * pieces], refs[2 * pieces :]
    query_ref, query_at_ref, query_cos_ref, query_sin_ref, *tables = refs[:8]
    turned, top, mass, total, cached_buf, fresh_buf, keys_buf, values_buf, sems = refs[8:]
    slots, _, columns = query_ref.shape
    span, width = cached_buf.shape[-2:]
    group = columns // width
    stretches = slot_ref.shape[0]
    last = functools.reduce(jnp.maximum, [place_ref[s] for s in range(slots)])

    def there(position):
        places = locate(slot_ref[position], seq_ref[0], slot_ref)
        return functools.reduce(jnp.logical_or, [place[0] for place in places])

    def copies(position, act):
        places = locate(slot_ref[position], seq_ref[0], slot_ref)
        fetch(act, places, cached, fresh, cached_buf, fresh_buf, sems, position)

    def start(position, carry):
        copies(position, lambda copy: copy.start())

        @pl.when(jnp.logical_not(there(position)))
        def _():
            cached_buf[position] = jnp.zeros_like(cached_buf[position])
            fresh_buf[position] = jnp.zeros_like(fresh_buf[position])

        return carry

    lax.fori_loop(0, last + 1, start, 0)

    def prepare(slot, carry):
        @pl.when(place_ref[slot] >= 0)
        def _():
            cosine, sine = query_cos_ref[slot], query_sin_ref[slot]
            heads = [
                turn(query_ref[slot, :, h * width : (h + 1) * width].astype(jnp.float32), cosine, sine)
                for h in range(group)
            ]
            turned[slot] = jnp.concatenate(heads, 0).astype(jnp.bfloat16)

        return carry

    lax.fori_loop(0, slots, prepare, 0)
    index = lax.broadcasted_iota(jnp.int32, (rows, span), 1)

    def wall(slot, position):
        limit = query_at_ref[slot] - position * span
        limit = jnp.concatenate([limit] * (span // width), 1)
        end = jnp.where(there(position), length_ref[position] - 1, -1)
        return jnp.where(index <= jnp.minimum(limit, end), 0.0, FAR)

    if stretches <= 4:
        for count in range(1, stretches + 1):

            @pl.when(last == count - 1)
            def _(count=count):
                for position in range(count):
                    copies(position, lambda copy: copy.wait())
                for position in range(count):
                    here = slice(position * span, (position + 1) * span)
                    keys_buf[here], values_buf[here] = ready(
                        cached_buf.at[position], fresh_buf.at[position], position, rows, tables
                    )

        def one(slot, carry):
            for count in range(1, stretches + 1):

                @pl.when(place_ref[slot] == count - 1)
                def _(count=count):
                    walls = [wall(slot, position) for position in range(count)]
                    walls = jnp.concatenate([jnp.concatenate(walls, 1)] * group, 0)
                    scores = score(turned[slot], keys_buf[: count * span]) + walls
                    highest = jnp.max(scores, 1, keepdims=True)
                    weight = jnp.exp2((scores - highest) * factor)
                    shape = top.shape[1:]
                    top[slot] = jnp.broadcast_to(highest, shape)
                    mass[slot] = jnp.broadcast_to(jnp.sum(weight, 1, keepdims=True), shape)
                    total[slot] = jnp.dot(
                        weight.astype(jnp.bfloat16),
                        values_buf[: count * span],
                        preferred_element_type=jnp.float32,
                    )

            return carry

        lax.fori_loop(0, slots, one, 0)
        return

    def stretch(position, carry):
        copies(position, lambda copy: copy.wait())
        keys_buf[:span], values_buf[:span] = ready(
            cached_buf.at[position], fresh_buf.at[position], position, rows, tables
        )

        def one(slot, carry):
            @pl.when(place_ref[slot] >= position)
            def _():
                walls = jnp.concatenate([wall(slot, position)] * group, 0)
                scores = score(turned[slot], keys_buf[:span]) + walls
                state = [ref.at[slot] for ref in (top, mass, total)]
                absorb(position == 0, state, scores, values_buf[:span], factor)

            return carry

        return lax.fori_loop(0, slots, one, carry)

    lax.fori_loop(0, last + 1, stretch, 0)


def late_body(exchanged, rows, factor, slot_ref, length_ref, place_ref, seq_ref, *refs):
    if exchanged:
        message, fresh, *tables = refs[:6]
        refs = refs[6:]
    query_at_ref, turned, early_top, early_mass, early_total, out_ref, keys_buf, values_buf = refs
    slots, _, columns = out_ref.shape
    width = turned.shape[-1]
    group = columns // width

    def write(slot, result):
        for head in range(group):
            mine = result[head * rows : (head + 1) * rows]
            out_ref[slot, :, head * width : (head + 1) * width] = mine.astype(jnp.bfloat16)

    def plain(slot):
        write(slot, early_total[slot] / early_mass[slot])

    for slot in range(slots):

        @pl.when(place_ref[slot] < 0)
        def _(slot=slot):
            out_ref[slot] = jnp.zeros_like(out_ref[slot])

    if not exchanged:
        for slot in range(slots):
            pl.when(place_ref[slot] >= 0)(functools.partial(plain, slot))
        return

    _, _, span, _ = message.shape
    seq = seq_ref[0]
    chosen = far_slots(seq, slot_ref)
    places = [place_of(slot, slot_ref) for slot in chosen]
    for k, slot in enumerate(chosen):
        @pl.when(slot >= 0)
        def _(k=k, slot=slot):
            keys_buf[k], values_buf[k] = ready(
                message.at[slot % 2], fresh.at[slot % 2], places[k], rows, tables
            )

    index = lax.broadcasted_iota(jnp.int32, (1, span), 1)

    def settle(slot, count):
        scores = []
        for k in range(count):
            end = jnp.where(places[k] < place_ref[slot], length_ref[places[k]], 0)
            scores.append(score(turned[slot], keys_buf[k]) + jnp.where(index < end, 0.0, FAR))
        scores = jnp.concatenate(scores, 1)
        before = early_top[slot]
        after = jnp.maximum(before, jnp.max(scores, 1, keepdims=True))
        fade = jnp.exp2((before - after) * factor)
        weight = jnp.exp2((scores - after[:, :1]) * factor)
        mass = early_mass[slot] * fade + jnp.sum(weight, 1, keepdims=True)
        values = values_buf[:count].reshape(count * span, width)
        added = jnp.dot(weight.astype(jnp.bfloat16), values, preferred_element_type=jnp.float32)
        write(slot, (early_total[slot] * fade + added) / mass)

    count = jnp.where(chosen[1] >= 0, 2, jnp.where(chosen[0] >= 0, 1, 0))
    for slot in range(slots):
        for cases, act in ((0, plain), (1, functools.partial(settle, count=1)), (2, functools.partial(settle, count=2))):
            pl.when((place_ref[slot] >= 0) & (count == cases))(functools.partial(act, slot))


def attend(body, lists, far, near, out_shape, scratch, cost):
    specs = [pl.BlockSpec(memory_space=SMEM)] * len(lists)
    specs += [pl.BlockSpec(memory_space=pl.ANY)] * len(far)
    specs += [pl.BlockSpec(memory_space=VMEM)] * len(near)
    return pl.pallas_call(
        body,
        out_shape=out_shape,
        in_specs=specs,
        out_specs=jax.tree.map(lambda _: pl.BlockSpec(memory_space=VMEM), out_shape),
        scratch_shapes=scratch,
        cost_estimate=pl.CostEstimate(flops=cost, bytes_accessed=1000, transcendentals=0),
        compiler_params=pltpu.CompilerParams(vmem_limit_bytes=32 << 20),
        name=body.func.__name__,
    )(*lists, *far, *near)


def locate_all(slot, seq, slot_ref):
    return [(slot >= 0, (0, slot), (0, slot))]


def locate_early(slot, seq, slot_ref):
    away, index = (slot // 2) ^ seq, slot % 2
    at_end = outer(seq)
    near = [((away == 1) & (at_end == k), (2 - k, index), (1, index)) for k in range(2)]
    next_but_one = [((away == 2) & (at_end == k), (1 + k, index), (2, index)) for k in range(2)]
    return [(away == 0, (0, index), (0, index))] + near + next_but_one


def local(
    pool_kv, hidden_rows, norm_gain, kv_weight, queries, stretch_slot, stretch_lengths, recompute_rows
):
    slots, _, span, width = pool_kv.shape
    rows = recompute_rows.shape[1]
    stretches = stretch_slot.shape[0]
    seq_count = lax.axis_size("seq")
    seq = lax.axis_index("seq")
    parts = lax.axis_size(FEATURES)
    me = lax.axis_index(FEATURES)
    features = hidden_rows.shape[2] * parts
    exchanged = seq_count == 4 and slots == 2 and stretches <= 4
    padded = round_up(rows + 1, 16)

    def along_seq(value, distance):
        return lax.ppermute(value, "seq", [(z, z ^ distance) for z in range(seq_count)])

    first, second = [(0, 2), (3, 1), (1, 0), (2, 3)], [(1, 3), (2, 0), (0, 1), (3, 2)]

    if exchanged:
        one, two = [lax.ppermute(pool_kv, "seq", pairs) for pairs in (first, second)]

    marks = jnp.pad(recompute_rows.astype(jnp.float32), ((0, 0), (0, width - rows)), constant_values=-1.0)

    pieces = project(me.reshape(1), hidden_rows, norm_gain, kv_weight, parts)
    sums = [hold(pieces[0])]
    for distance in range(parts - 1, 0, -1):
        swap = [(i, i ^ distance) for i in range(parts)]
        sums.append(lax.ppermute(pieces[distance], FEATURES, swap))
    fresh_kv, payload = finish(sums, marks, slots, rows, width, features)

    mine = seq * slots + jnp.arange(slots, dtype=jnp.int32)
    hits = stretch_slot[:, None] == mine[None]
    order = jnp.arange(stretches, dtype=jnp.int32)[:, None]
    my_pos = jnp.max(jnp.where(hits, order, -1), 0)
    query_at = my_pos[:, None] * span + recompute_rows
    inverse = THETA ** (-2.0 * np.arange(width // 2) / width)
    inverse = np.concatenate([inverse, inverse]).astype(np.float32)
    angle = query_at.astype(jnp.float32)[..., None] * inverse
    flip = np.where(np.arange(width) < width // 2, -1.0, 1.0).astype(np.float32)
    query_tables = (
        jnp.broadcast_to(query_at[..., None], (slots, rows, width)),
        jnp.cos(angle),
        jnp.sin(angle) * flip,
    )
    tables = (*rope_tables(np.arange(span), width), *rope_tables(np.arange(stretches) * span, width))

    if exchanged:
        payloads = [payload, along_seq(payload, 1), along_seq(payload, 2)]
        message = assemble(seq.reshape(1), one, two, payload)
        early, locate = ([pool_kv, one, two], payloads), locate_early
        late = (along_seq(message, 1), along_seq(hold(payloads[2], message), 1), *tables)
    else:
        early = [[lax.all_gather(array, "seq", axis=0, tiled=True)] for array in (pool_kv, payload)]
        locate, late = locate_all, ()

    lists = (stretch_slot, stretch_lengths, my_pos, seq.reshape(1))
    lines = rows * (queries.shape[2] // width)
    factor = width ** (-0.5) * math.log2(math.e)
    state = (slots, lines, width)
    stage = pltpu.VMEM(((stretches if stretches <= 4 else 1) * span, width), jnp.bfloat16)
    passed = attend(
        functools.partial(early_body, len(early[0]), locate, rows, factor),
        lists,
        (*early[0], *early[1]),
        (queries, *query_tables, *tables),
        [jax.ShapeDtypeStruct(state, jnp.bfloat16)] + [jax.ShapeDtypeStruct(state, jnp.float32)] * 3,
        [
            pltpu.VMEM((stretches, 2, span, width), jnp.bfloat16),
            pltpu.VMEM((stretches, 2, padded, width), jnp.bfloat16),
            stage,
            stage,
            pltpu.SemaphoreType.DMA((stretches, 2)),
        ],
        EARLY_COST,
    )
    attended = attend(
        functools.partial(late_body, exchanged, rows, factor),
        lists,
        (),
        (*late, query_tables[0], *passed),
        jax.ShapeDtypeStruct(queries.shape, jnp.bfloat16),
        [
            pltpu.VMEM((2, span, width), jnp.bfloat16),
            pltpu.VMEM((2, span, width), jnp.bfloat16),
        ],
        1000,
    )
    return fresh_kv, attended


def solution(mesh):
    in_specs = (
        P(("groups", "seq"), None, None, FEATURES),
        P(("groups", "seq"), None, FEATURES),
        P(FEATURES),
        P(FEATURES, None),
        P(("groups", "seq"), None, FEATURES),
        P("groups"),
        P("groups"),
        P(("groups", "seq"), None),
    )
    out_specs = (
        P(("groups", "seq"), None, None, FEATURES),
        P(("groups", "seq"), None, FEATURES),
    )
    return jax.shard_map(local, mesh=mesh, in_specs=in_specs, out_specs=out_specs, check_vma=False)
```

```python
import functools
import math

import jax
import jax.numpy as jnp
import numpy as np
from jax import lax
from jax.experimental import pallas as pl
from jax.experimental.pallas import tpu as pltpu
from jax.sharding import PartitionSpec as P

THETA = 500000.0
EPS = 1e-05
FAR = -1e30
FEATURES = ("tp", "kvh")
VMEM = pltpu.MemorySpace.VMEM
SMEM = pltpu.MemorySpace.SMEM
PROJECT_VMEM = 61 << 20
EARLY_COST = 3*10**9


def round_up(value, step):
    return -(-value // step) * step


def rope_tables(positions, width):
    inverse = THETA ** (-2.0 * np.arange(width // 2) / width)
    angle = np.asarray(positions, np.float64)[:, None] * np.concatenate([inverse, inverse])[None]
    return np.cos(angle).astype(np.float32), np.sin(angle).astype(np.float32)


def turn(values, cosine, sine):
    return values * cosine + pltpu.roll(values, values.shape[-1] // 2, 1) * sine


def place_of(slot, slot_ref):
    place = jnp.int32(-1)
    for position in range(slot_ref.shape[0]):
        place = jnp.where(slot_ref[position] == slot, jnp.int32(position), place)
    return place


def outer(seq):
    return jnp.where((seq == 0) | (seq == 3), 1, 0)


def far_slots(seq, slot_ref):
    last = jnp.maximum(*[place_of(2 * seq + j, slot_ref) for j in range(2)])
    slots = [2 * (seq ^ 3) + j for j in range(2)]
    slots = [jnp.where(place_of(slot, slot_ref) < last, slot, -1) for slot in slots]
    slots = [jnp.where(place_of(slot, slot_ref) < 0, -1, slot) for slot in slots]
    return [jnp.where(slots[0] >= 0, slots[0], slots[1]), jnp.where(slots[0] >= 0, slots[1], -1)]


def project_body(ks, me_ref, hidden_ref, gain_ref, weight_ref, *refs):
    *pieces, held, gain, weights, sems = refs
    slots, rows, features = held.shape
    count = slots * rows
    height, columns = pieces[0].shape
    spare = height - count

    def block(at, k):
        first = pl.multiple_of((me_ref[0] ^ k) * columns, columns)
        part = weight_ref.at[:, pl.ds(first, columns)]
        return pltpu.make_async_copy(part, weights.at[at], sems.at[2 + at])

    arrive = pltpu.make_async_copy(hidden_ref, held, sems.at[0])
    follow = pltpu.make_async_copy(gain_ref, gain, sems.at[1])
    arrive.start()
    follow.start()
    for at, k in enumerate(ks):
        block(at, k).start()
    arrive.wait()
    follow.wait()
    hidden = held[...].astype(jnp.float32).reshape(count, features)
    scaled = (hidden * gain[...].astype(jnp.float32).reshape(1, features)).astype(jnp.bfloat16)
    square = hidden * hidden
    fill = jnp.zeros((round_up(count, 128) - count, features), jnp.float32)
    square = jnp.concatenate([square, fill], 0)
    high = square.astype(jnp.bfloat16)
    low = (square - high.astype(jnp.float32)).astype(jnp.bfloat16)
    ones = jnp.ones((spare, features), jnp.bfloat16)
    along = (((1,), (1,)), ((), ()))
    total = lax.dot_general(ones, high, along, preferred_element_type=jnp.float32)
    total += lax.dot_general(ones, low, along, preferred_element_type=jnp.float32)
    coarse = total.astype(jnp.bfloat16).astype(jnp.float32)
    row = lax.broadcasted_iota(jnp.int32, total.shape, 0)
    both = jnp.where(row == 0, coarse, jnp.where(row == 1, total - coarse, 0.0))
    rest = jnp.zeros((spare, columns - total.shape[1]), jnp.float32)
    tail = jnp.concatenate([both, rest], 1).astype(jnp.bfloat16)
    for at, k in enumerate(ks):
        block(at, k).wait()
        product = jnp.dot(scaled, weights[at], preferred_element_type=jnp.float32)
        pieces[at][:count] = product.astype(jnp.bfloat16)
        pieces[at][count:] = tail


def project(me, hidden_rows, norm_gain, kv_weight, parts, ks):
    slots, rows, features = hidden_rows.shape
    columns = kv_weight.shape[1] // parts
    shape = (slots * rows + 16, columns)
    return pl.pallas_call(
        functools.partial(project_body, ks),
        out_shape=[jax.ShapeDtypeStruct(shape, jnp.bfloat16)] * len(ks),
        in_specs=[pl.BlockSpec(memory_space=SMEM)] + [pl.BlockSpec(memory_space=pltpu.HBM)] * 3,
        out_specs=[pl.BlockSpec(memory_space=VMEM)] * len(ks),
        scratch_shapes=[
            pltpu.VMEM(hidden_rows.shape, jnp.bfloat16),
            pltpu.VMEM(norm_gain.shape, jnp.bfloat16),
            pltpu.VMEM((len(ks), features, columns), jnp.bfloat16),
            pltpu.SemaphoreType.DMA((2 + len(ks),)),
        ],
        cost_estimate=pl.CostEstimate(flops=1000, bytes_accessed=1000, transcendentals=0),
        compiler_params=pltpu.CompilerParams(vmem_limit_bytes=PROJECT_VMEM),
        name="project",
    )(me, hidden_rows, norm_gain, kv_weight)


def finish_body(features, rows, marks_ref, *refs):
    *pieces, payload_ref = refs
    slots, _, padded, width = payload_ref.shape
    count = slots * rows
    total = pieces[0][...].astype(jnp.float32)
    for piece in pieces[1:]:
        total += piece[...].astype(jnp.float32)
    lanes = round_up(count, 128)
    squares = total[count : count + 1, :lanes] + total[count + 1 : count + 2, :lanes]
    inverse = lax.rsqrt(squares / features + EPS)
    inverse = jnp.transpose(jnp.broadcast_to(inverse, (lanes, lanes)))[:count, :width]
    for half in range(2):
        values = total[:count, half * width : (half + 1) * width] * inverse
        for slot in range(slots):
            mine = values[slot * rows : (slot + 1) * rows]
            marks = jnp.broadcast_to(marks_ref[slot : slot + 1], (padded - rows, width))
            marked = jnp.concatenate([mine, marks], 0)
            payload_ref[slot, half] = marked.astype(jnp.bfloat16)


def finish(pieces, marks, slots, rows, width, features):
    shape = (slots, 2, round_up(rows + 1, 16), width)
    return pl.pallas_call(
        functools.partial(finish_body, features, rows),
        out_shape=jax.ShapeDtypeStruct(shape, jnp.bfloat16),
        cost_estimate=pl.CostEstimate(flops=1000, bytes_accessed=1000, transcendentals=0),
        compiler_params=pltpu.CompilerParams(vmem_limit_bytes=8 << 20),
        name="finish",
    )(marks, *pieces)


def assemble_body(seq_ref, one_ref, two_ref, ahead_ref, out_ref, sem):
    del ahead_ref
    at_end = outer(seq_ref[0])
    for wanted, ref in ((0, one_ref), (1, two_ref)):

        @pl.when(at_end == wanted)
        def _(ref=ref):
            copy = pltpu.make_async_copy(ref, out_ref, sem)
            copy.start()
            copy.wait()


def assemble(seq, one, two, ahead):
    far = pl.BlockSpec(memory_space=pl.ANY)
    return pl.pallas_call(
        assemble_body,
        out_shape=jax.ShapeDtypeStruct(one.shape, one.dtype),
        in_specs=[pl.BlockSpec(memory_space=SMEM), far, far, far],
        out_specs=pl.BlockSpec(memory_space=VMEM),
        scratch_shapes=[pltpu.SemaphoreType.DMA(())],
        cost_estimate=pl.CostEstimate(flops=1000, bytes_accessed=1000, transcendentals=0),
        compiler_params=pltpu.CompilerParams(vmem_limit_bytes=8 << 20),
        name="assemble",
    )(seq, one, two, ahead)


def hold_body(value_ref, *refs):
    refs[-1][...] = value_ref[...]


def hold(value, *ahead):
    near, far = pl.BlockSpec(memory_space=VMEM), pl.BlockSpec(memory_space=pl.ANY)
    return pl.pallas_call(
        hold_body,
        out_shape=jax.ShapeDtypeStruct(value.shape, value.dtype),
        in_specs=[near] + [far] * len(ahead),
        out_specs=near,
        cost_estimate=pl.CostEstimate(flops=1000, bytes_accessed=1000, transcendentals=0),
        compiler_params=pltpu.CompilerParams(vmem_limit_bytes=8 << 20),
        name="hold",
    )(value, *ahead)


def ready(cached, fresh, position, rows, tables):
    cos_ref, sin_ref, base_cos_ref, base_sin_ref = tables
    _, span, width = cached.shape
    start = rows - rows % 16
    marks = fresh[0, start:].astype(jnp.float32)[rows - start : rows - start + 1]
    token = lax.broadcasted_iota(jnp.int32, (span, width), 0).astype(jnp.float32)
    chosen = jnp.where(token == marks, 1.0, 0.0).astype(jnp.bfloat16)[:, : fresh.shape[-2]]
    keys, values = fresh[0], fresh[1]
    source = jnp.concatenate([keys, values, jnp.ones_like(keys)], 1)
    placed = jnp.dot(chosen, source, preferred_element_type=jnp.float32)
    replaced = placed[:, 2 * width :] > 0.5
    old_keys, old_values = cached[0], cached[1]
    keys = jnp.where(replaced, placed[:, :width], old_keys.astype(jnp.float32))
    values = jnp.where(replaced, placed[:, width : 2 * width], old_values.astype(jnp.float32))
    base_cos, base_sin = base_cos_ref[pl.ds(position, 1)], base_sin_ref[pl.ds(position, 1)]
    flip = jnp.where(lax.broadcasted_iota(jnp.int32, (1, width), 1) < width // 2, -1.0, 1.0)
    cosine = cos_ref[...] * base_cos - sin_ref[...] * base_sin
    sine = (sin_ref[...] * base_cos + cos_ref[...] * base_sin) * flip
    return turn(keys, cosine, sine).astype(jnp.bfloat16), values.astype(jnp.bfloat16)


def fetch(act, places, cached, fresh, cached_buf, fresh_buf, sems, position):
    for wanted, *sources in places:

        @pl.when(wanted)
        def _(sources=sources):
            for which, refs, buf in ((0, cached, cached_buf), (1, fresh, fresh_buf)):
                piece, index = sources[which]
                act(
                    pltpu.make_async_copy(
                        refs[piece].at[index], buf.at[position], sems.at[position, which]
                    )
                )


def score(query, keys):
    along = (((1,), (1,)), ((), ()))
    return lax.dot_general(query, keys, along, preferred_element_type=jnp.float32)


def absorb(first, state, scores, values, factor):
    top, mass, total = state
    before = jnp.where(first, FAR, top[...])
    after = jnp.maximum(before, jnp.max(scores, 1, keepdims=True))
    fade = jnp.where(first, 0.0, jnp.exp2((before - after) * factor))
    weight = jnp.exp2((scores - after[:, :1]) * factor)
    top[...] = after
    mass[...] = jnp.where(first, 0.0, mass[...]) * fade + jnp.sum(weight, 1, keepdims=True)
    total[...] = jnp.where(first, 0.0, total[...]) * fade + jnp.dot(
        weight.astype(jnp.bfloat16), values, preferred_element_type=jnp.float32
    )


def early_body(pieces, locate, rows, factor, slot_ref, length_ref, place_ref, seq_ref, *refs):
    cached, fresh, refs = refs[:pieces], refs[pieces : 2 * pieces], refs[2 * pieces :]
    payload_ref, query_ref, query_at_ref, query_cos_ref, query_sin_ref, *tables = refs[:9]
    turned, top, mass, total, facts, mine_ref, cached_buf, fresh_buf, keys_buf, values_buf, sems = refs[9:]
    slots, _, columns = query_ref.shape
    span, width = cached_buf.shape[-2:]
    group = columns // width
    stretches = slot_ref.shape[0]
    last = functools.reduce(jnp.maximum, [place_ref[s] for s in range(slots)])
    for slot in range(slots):
        for half in range(2):
            mine_ref[slot, half] = payload_ref[slot, half].astype(jnp.float32)[:rows].astype(jnp.bfloat16)
    chosen = far_slots(seq_ref[0], slot_ref) if pieces > 1 else []
    known = []
    for slot in chosen:
        place = place_of(slot, slot_ref)
        end = jnp.where(place >= 0, length_ref[jnp.maximum(place, 0)], 0)
        known += [jnp.where(slot >= 0, slot % 2, -1), place, end]
    known = [place_ref[slot] for slot in range(slots)] + known
    lane = lax.broadcasted_iota(jnp.int32, facts.shape, 1)
    line = jnp.zeros(facts.shape, jnp.int32)
    for k, value in enumerate(known):
        line = jnp.where(lane == k, value, line)
    facts[...] = line

    def there(position):
        places = locate(slot_ref[position], seq_ref[0], slot_ref)
        return functools.reduce(jnp.logical_or, [place[0] for place in places])

    def copies(position, act):
        places = locate(slot_ref[position], seq_ref[0], slot_ref)
        fetch(act, places, cached, fresh, cached_buf, fresh_buf, sems, position)

    def start(position, carry):
        copies(position, lambda copy: copy.start())

        @pl.when(jnp.logical_not(there(position)))
        def _():
            cached_buf[position] = jnp.zeros_like(cached_buf[position])
            fresh_buf[position] = jnp.zeros_like(fresh_buf[position])

        return carry

    lax.fori_loop(0, last + 1, start, 0)

    def prepare(slot, carry):
        @pl.when(place_ref[slot] >= 0)
        def _():
            cosine, sine = query_cos_ref[slot], query_sin_ref[slot]
            heads = [
                turn(query_ref[slot, :, h * width : (h + 1) * width].astype(jnp.float32), cosine, sine)
                for h in range(group)
            ]
            turned[slot] = jnp.concatenate(heads, 0).astype(jnp.bfloat16)

        return carry

    lax.fori_loop(0, slots, prepare, 0)
    index = lax.broadcasted_iota(jnp.int32, (rows, span), 1)

    def wall(slot, position):
        limit = query_at_ref[slot] - position * span
        limit = jnp.concatenate([limit] * (span // width), 1)
        end = jnp.where(there(position), length_ref[position] - 1, -1)
        return jnp.where(index <= jnp.minimum(limit, end), 0.0, FAR)

    if stretches <= 4:
        for count in range(1, stretches + 1):

            @pl.when(last == count - 1)
            def _(count=count):
                for position in range(count):
                    copies(position, lambda copy: copy.wait())
                for position in range(count):
                    here = slice(position * span, (position + 1) * span)
                    keys_buf[here], values_buf[here] = ready(
                        cached_buf.at[position], fresh_buf.at[position], position, rows, tables
                    )

        def one(slot, carry):
            for count in range(1, stretches + 1):

                @pl.when(place_ref[slot] == count - 1)
                def _(count=count):
                    walls = [wall(slot, position) for position in range(count)]
                    walls = jnp.concatenate([jnp.concatenate(walls, 1)] * group, 0)
                    scores = score(turned[slot], keys_buf[: count * span]) + walls
                    highest = jnp.max(scores, 1, keepdims=True)
                    weight = jnp.exp2((scores - highest) * factor)
                    shape = top.shape[1:]
                    top[slot] = jnp.broadcast_to(highest, shape)
                    mass[slot] = jnp.broadcast_to(jnp.sum(weight, 1, keepdims=True), shape)
                    total[slot] = jnp.dot(
                        weight.astype(jnp.bfloat16),
                        values_buf[: count * span],
                        preferred_element_type=jnp.float32,
                    )

            return carry

        lax.fori_loop(0, slots, one, 0)
        return

    def stretch(position, carry):
        copies(position, lambda copy: copy.wait())
        keys_buf[:span], values_buf[:span] = ready(
            cached_buf.at[position], fresh_buf.at[position], position, rows, tables
        )

        def one(slot, carry):
            @pl.when(place_ref[slot] >= position)
            def _():
                walls = jnp.concatenate([wall(slot, position)] * group, 0)
                scores = score(turned[slot], keys_buf[:span]) + walls
                state = [ref.at[slot] for ref in (top, mass, total)]
                absorb(position == 0, state, scores, values_buf[:span], factor)

            return carry

        return lax.fori_loop(0, slots, one, carry)

    lax.fori_loop(0, last + 1, stretch, 0)


def late_body(exchanged, rows, factor, *refs):
    if exchanged:
        message, fresh, *tables = refs[:6]
        refs = refs[6:]
    turned, early_top, early_mass, early_total, facts, out_ref, *refs = refs
    out_buf, keys_buf, values_buf, sems = refs
    slots, _, columns = out_buf.shape
    width = turned.shape[-1]
    group = columns // width
    mine = [facts[0, slot] for slot in range(slots)]

    def write(slot, result):
        for head in range(group):
            part = result[head * rows : (head + 1) * rows]
            out_buf[slot, :, head * width : (head + 1) * width] = part.astype(jnp.bfloat16)

    def leave(slot):
        return pltpu.make_async_copy(out_buf.at[slot], out_ref.at[slot], sems.at[slot])

    chosen = [[facts[0, slots + 3 * k + j] for j in range(3)] for k in range(2)] if exchanged else []
    touched = [
        functools.reduce(
            jnp.logical_or, [(at >= 0) & (place < mine[slot]) for at, place, _ in chosen], jnp.bool_(False)
        )
        for slot in range(slots)
    ]
    for slot in range(slots):

        @pl.when(mine[slot] < 0)
        def _(slot=slot):
            out_buf[slot] = jnp.zeros_like(out_buf[slot])
            leave(slot).start()

        @pl.when((mine[slot] >= 0) & jnp.logical_not(touched[slot]))
        def _(slot=slot):
            write(slot, early_total[slot] / early_mass[slot])
            leave(slot).start()

    def settle(slot, count):
        span = message.shape[2]
        index = lax.broadcasted_iota(jnp.int32, (1, span), 1)
        scores = []
        for k in range(count):
            _, place, length = chosen[k]
            end = jnp.where(place < mine[slot], length, 0)
            scores.append(score(turned[slot], keys_buf[k]) + jnp.where(index < end, 0.0, FAR))
        scores = jnp.concatenate(scores, 1)
        before = early_top[slot]
        after = jnp.maximum(before, jnp.max(scores, 1, keepdims=True))
        fade = jnp.exp2((before - after) * factor)
        weight = jnp.exp2((scores - after[:, :1]) * factor)
        mass = early_mass[slot] * fade + jnp.sum(weight, 1, keepdims=True)
        values = values_buf[:count].reshape(count * span, width)
        added = jnp.dot(weight.astype(jnp.bfloat16), values, preferred_element_type=jnp.float32)
        write(slot, (early_total[slot] * fade + added) / mass)

    def take(count):
        for k in range(count):
            at, place, _ = chosen[k]
            keys_buf[k], values_buf[k] = ready(message.at[at], fresh.at[at], place, rows, tables)
        for slot in range(slots):

            @pl.when(touched[slot])
            def _(slot=slot):
                settle(slot, count)
                leave(slot).start()

    if exchanged:
        pl.when((chosen[0][0] >= 0) & (chosen[1][0] < 0))(functools.partial(take, 1))
        pl.when(chosen[1][0] >= 0)(functools.partial(take, 2))
    for slot in range(slots):
        leave(slot).wait()


def attend(body, lists, far, near, out_shape, out_space, scratch, cost):
    specs = [pl.BlockSpec(memory_space=SMEM)] * len(lists)
    specs += [pl.BlockSpec(memory_space=pl.ANY)] * len(far)
    specs += [pl.BlockSpec(memory_space=VMEM)] * len(near)
    return pl.pallas_call(
        body,
        out_shape=out_shape,
        in_specs=specs,
        out_specs=jax.tree.map(lambda _: pl.BlockSpec(memory_space=out_space), out_shape),
        scratch_shapes=scratch,
        cost_estimate=pl.CostEstimate(flops=cost, bytes_accessed=1000, transcendentals=0),
        compiler_params=pltpu.CompilerParams(vmem_limit_bytes=32 << 20),
        name=body.func.__name__,
    )(*lists, *far, *near)


def locate_all(slot, seq, slot_ref):
    return [(slot >= 0, (0, slot), (0, slot))]


def locate_early(slot, seq, slot_ref):
    away, index = (slot // 2) ^ seq, slot % 2
    at_end = outer(seq)
    near = [((away == 1) & (at_end == k), (2 - k, index), (1, index)) for k in range(2)]
    next_but_one = [((away == 2) & (at_end == k), (1 + k, index), (2, index)) for k in range(2)]
    return [(away == 0, (0, index), (0, index))] + near + next_but_one


def local(
    pool_kv, hidden_rows, norm_gain, kv_weight, queries, stretch_slot, stretch_lengths, recompute_rows
):
    slots, _, span, width = pool_kv.shape
    rows = recompute_rows.shape[1]
    stretches = stretch_slot.shape[0]
    seq_count = lax.axis_size("seq")
    seq = lax.axis_index("seq")
    parts = lax.axis_size(FEATURES)
    me = lax.axis_index(FEATURES)
    features = hidden_rows.shape[2] * parts
    exchanged = seq_count == 4 and slots == 2 and stretches <= 4
    padded = round_up(rows + 1, 16)

    def along_seq(value, distance):
        return lax.ppermute(value, "seq", [(z, z ^ distance) for z in range(seq_count)])

    first, second = [(0, 2), (3, 1), (1, 0), (2, 3)], [(1, 3), (2, 0), (0, 1), (3, 2)]

    if exchanged:
        one, two = [lax.ppermute(pool_kv, "seq", pairs) for pairs in (first, second)]

    marks = jnp.pad(recompute_rows.astype(jnp.float32), ((0, 0), (0, width - rows)), constant_values=-1.0)

    def part(ks):
        return project(me.reshape(1), hidden_rows, norm_gain, kv_weight, parts, ks)

    def hand(piece, distance):
        return lax.ppermute(piece, FEATURES, [(i, i ^ distance) for i in range(parts)])

    away = tuple(range(parts - 1, 1, -1))
    sums = [hand(piece, distance) for piece, distance in zip(part(away), away)]
    near, own = part((1, 0))
    sums += [hand(near, 1), hold(own)]

    payload = finish(sums, marks, slots, rows, width, features)

    mine = seq * slots + jnp.arange(slots, dtype=jnp.int32)
    hits = stretch_slot[:, None] == mine[None]
    order = jnp.arange(stretches, dtype=jnp.int32)[:, None]
    my_pos = jnp.max(jnp.where(hits, order, -1), 0)
    query_at = my_pos[:, None] * span + recompute_rows
    inverse = THETA ** (-2.0 * np.arange(width // 2) / width)
    inverse = np.concatenate([inverse, inverse]).astype(np.float32)
    angle = query_at.astype(jnp.float32)[..., None] * inverse
    flip = np.where(np.arange(width) < width // 2, -1.0, 1.0).astype(np.float32)
    query_tables = (
        jnp.broadcast_to(query_at[..., None], (slots, rows, width)),
        jnp.cos(angle),
        jnp.sin(angle) * flip,
    )
    tables = (*rope_tables(np.arange(span), width), *rope_tables(np.arange(stretches) * span, width))

    if exchanged:
        payloads = [payload, along_seq(payload, 1), along_seq(payload, 2)]
        message = assemble(seq.reshape(1), one, two, payload)
        early, locate = ([pool_kv, one, two], payloads), locate_early
        late = (along_seq(message, 1), along_seq(hold(payloads[2], message), 1), *tables)
    else:
        early = [[lax.all_gather(array, "seq", axis=0, tiled=True)] for array in (pool_kv, payload)]
        locate, late = locate_all, ()

    lists = (stretch_slot, stretch_lengths, my_pos, seq.reshape(1))
    lines = rows * (queries.shape[2] // width)
    factor = width ** (-0.5) * math.log2(math.e)
    state = (slots, lines, width)
    stage = pltpu.VMEM(((stretches if stretches <= 4 else 1) * span, width), jnp.bfloat16)
    *passed, fresh_kv = attend(
        functools.partial(early_body, len(early[0]), locate, rows, factor),
        lists,
        (*early[0], *early[1]),
        (payload, queries, *query_tables, *tables),
        [jax.ShapeDtypeStruct(state, jnp.bfloat16)]
        + [jax.ShapeDtypeStruct(state, jnp.float32)] * 3
        + [jax.ShapeDtypeStruct((8, 128), jnp.int32)]
        + [jax.ShapeDtypeStruct((slots, 2, rows, width), jnp.bfloat16)],
        VMEM,
        [
            pltpu.VMEM((stretches, 2, span, width), jnp.bfloat16),
            pltpu.VMEM((stretches, 2, padded, width), jnp.bfloat16),
            stage,
            stage,
            pltpu.SemaphoreType.DMA((stretches, 2)),
        ],
        EARLY_COST,
    )
    attended = attend(
        functools.partial(late_body, exchanged, rows, factor),
        (),
        (),
        (*late, *passed),
        jax.ShapeDtypeStruct(queries.shape, jnp.bfloat16),
        pl.ANY,
        [
            pltpu.VMEM(queries.shape, jnp.bfloat16),
            pltpu.VMEM((2, span, width), jnp.bfloat16),
            pltpu.VMEM((2, span, width), jnp.bfloat16),
            pltpu.SemaphoreType.DMA((slots,)),
        ],
        1000,
    )
    return fresh_kv, attended


def solution(mesh):
    in_specs = (
        P(("groups", "seq"), None, None, FEATURES),
        P(("groups", "seq"), None, FEATURES),
        P(FEATURES),
        P(FEATURES, None),
        P(("groups", "seq"), None, FEATURES),
        P("groups"),
        P("groups"),
        P(("groups", "seq"), None),
    )
    out_specs = (
        P(("groups", "seq"), None, None, FEATURES),
        P(("groups", "seq"), None, FEATURES),
    )
    return jax.shard_map(local, mesh=mesh, in_specs=in_specs, out_specs=out_specs, check_vma=False)
```

```python
import functools
import math

import jax
import jax.numpy as jnp
import numpy as np
from jax import lax
from jax.experimental import pallas as pl
from jax.experimental.pallas import tpu as pltpu
from jax.sharding import PartitionSpec as P

THETA = 500000.0
EPS = 1e-05
FAR = -1e30
FEATURES = ("tp", "kvh")
VMEM = pltpu.MemorySpace.VMEM
SMEM = pltpu.MemorySpace.SMEM
PROJECT_VMEM = 61 << 20
EARLY_COST = 3*10**9


def round_up(value, step):
    return -(-value // step) * step


def rope_tables(positions, width):
    inverse = THETA ** (-2.0 * np.arange(width // 2) / width)
    angle = np.asarray(positions, np.float64)[:, None] * np.concatenate([inverse, inverse])[None]
    return np.cos(angle).astype(np.float32), np.sin(angle).astype(np.float32)


def turn(values, cosine, sine):
    return values * cosine + pltpu.roll(values, values.shape[-1] // 2, 1) * sine


def place_of(slot, slot_ref):
    place = jnp.int32(-1)
    for position in range(slot_ref.shape[0]):
        place = jnp.where(slot_ref[position] == slot, jnp.int32(position), place)
    return place


def outer(seq):
    return jnp.where((seq == 0) | (seq == 3), 0, 1)


def far_slots(seq, slot_ref):
    last = jnp.maximum(*[place_of(2 * seq + j, slot_ref) for j in range(2)])
    slots = [2 * (seq ^ 3) + j for j in range(2)]
    slots = [jnp.where(place_of(slot, slot_ref) < last, slot, -1) for slot in slots]
    slots = [jnp.where(place_of(slot, slot_ref) < 0, -1, slot) for slot in slots]
    return [jnp.where(slots[0] >= 0, slots[0], slots[1]), jnp.where(slots[0] >= 0, slots[1], -1)]


def project_body(ks, me_ref, hidden_ref, gain_ref, weight_ref, *refs):
    *pieces, held, gain, weights, sems = refs
    slots, rows, features = held.shape
    count = slots * rows
    height, columns = pieces[0].shape
    spare = height - count

    def block(at, k):
        first = pl.multiple_of((me_ref[0] ^ k) * columns, columns)
        part = weight_ref.at[:, pl.ds(first, columns)]
        return pltpu.make_async_copy(part, weights.at[at], sems.at[2 + at])

    arrive = pltpu.make_async_copy(hidden_ref, held, sems.at[0])
    follow = pltpu.make_async_copy(gain_ref, gain, sems.at[1])
    arrive.start()
    follow.start()
    for at, k in enumerate(ks):
        block(at, k).start()
    arrive.wait()
    follow.wait()
    hidden = held[...].astype(jnp.float32).reshape(count, features)
    scaled = (hidden * gain[...].astype(jnp.float32).reshape(1, features)).astype(jnp.bfloat16)
    square = hidden * hidden
    fill = jnp.zeros((round_up(count, 128) - count, features), jnp.float32)
    square = jnp.concatenate([square, fill], 0)
    high = square.astype(jnp.bfloat16)
    low = (square - high.astype(jnp.float32)).astype(jnp.bfloat16)
    ones = jnp.ones((spare, features), jnp.bfloat16)
    along = (((1,), (1,)), ((), ()))
    total = lax.dot_general(ones, high, along, preferred_element_type=jnp.float32)
    total += lax.dot_general(ones, low, along, preferred_element_type=jnp.float32)
    coarse = total.astype(jnp.bfloat16).astype(jnp.float32)
    row = lax.broadcasted_iota(jnp.int32, total.shape, 0)
    both = jnp.where(row == 0, coarse, jnp.where(row == 1, total - coarse, 0.0))
    rest = jnp.zeros((spare, columns - total.shape[1]), jnp.float32)
    tail = jnp.concatenate([both, rest], 1).astype(jnp.bfloat16)
    for at, k in enumerate(ks):
        block(at, k).wait()
        product = jnp.dot(scaled, weights[at], preferred_element_type=jnp.float32)
        pieces[at][:count] = product.astype(jnp.bfloat16)
        pieces[at][count:] = tail


def project(me, hidden_rows, norm_gain, kv_weight, parts, ks):
    slots, rows, features = hidden_rows.shape
    columns = kv_weight.shape[1] // parts
    shape = (slots * rows + 16, columns)
    return pl.pallas_call(
        functools.partial(project_body, ks),
        out_shape=[jax.ShapeDtypeStruct(shape, jnp.bfloat16)] * len(ks),
        in_specs=[pl.BlockSpec(memory_space=SMEM)] + [pl.BlockSpec(memory_space=pltpu.HBM)] * 3,
        out_specs=[pl.BlockSpec(memory_space=VMEM)] * len(ks),
        scratch_shapes=[
            pltpu.VMEM(hidden_rows.shape, jnp.bfloat16),
            pltpu.VMEM(norm_gain.shape, jnp.bfloat16),
            pltpu.VMEM((len(ks), features, columns), jnp.bfloat16),
            pltpu.SemaphoreType.DMA((2 + len(ks),)),
        ],
        cost_estimate=pl.CostEstimate(flops=1000, bytes_accessed=1000, transcendentals=0),
        compiler_params=pltpu.CompilerParams(vmem_limit_bytes=PROJECT_VMEM),
        name="project",
    )(me, hidden_rows, norm_gain, kv_weight)


def finish_body(features, rows, marks_ref, *refs):
    *pieces, payload_ref = refs
    slots, _, padded, width = payload_ref.shape
    count = slots * rows
    total = pieces[0][...].astype(jnp.float32)
    for piece in pieces[1:]:
        total += piece[...].astype(jnp.float32)
    lanes = round_up(count, 128)
    squares = total[count : count + 1, :lanes] + total[count + 1 : count + 2, :lanes]
    inverse = lax.rsqrt(squares / features + EPS)
    inverse = jnp.transpose(jnp.broadcast_to(inverse, (lanes, lanes)))[:count, :width]
    for half in range(2):
        values = total[:count, half * width : (half + 1) * width] * inverse
        for slot in range(slots):
            mine = values[slot * rows : (slot + 1) * rows]
            marks = jnp.broadcast_to(marks_ref[slot : slot + 1], (padded - rows, width))
            marked = jnp.concatenate([mine, marks], 0)
            payload_ref[slot, half] = marked.astype(jnp.bfloat16)


def finish(pieces, marks, slots, rows, width, features):
    shape = (slots, 2, round_up(rows + 1, 16), width)
    return pl.pallas_call(
        functools.partial(finish_body, features, rows),
        out_shape=jax.ShapeDtypeStruct(shape, jnp.bfloat16),
        cost_estimate=pl.CostEstimate(flops=1000, bytes_accessed=1000, transcendentals=0),
        compiler_params=pltpu.CompilerParams(vmem_limit_bytes=8 << 20),
        name="finish",
    )(marks, *pieces)


def assemble_body(seq_ref, one_ref, two_ref, ahead_ref, out_ref, sem):
    del ahead_ref
    at_end = outer(seq_ref[0])
    for wanted, ref in ((0, one_ref), (1, two_ref)):

        @pl.when(at_end == wanted)
        def _(ref=ref):
            copy = pltpu.make_async_copy(ref, out_ref, sem)
            copy.start()
            copy.wait()


def assemble(seq, one, two, ahead):
    far = pl.BlockSpec(memory_space=pl.ANY)
    return pl.pallas_call(
        assemble_body,
        out_shape=jax.ShapeDtypeStruct(one.shape, one.dtype),
        in_specs=[pl.BlockSpec(memory_space=SMEM), far, far, far],
        out_specs=pl.BlockSpec(memory_space=VMEM),
        scratch_shapes=[pltpu.SemaphoreType.DMA(())],
        cost_estimate=pl.CostEstimate(flops=1000, bytes_accessed=1000, transcendentals=0),
        compiler_params=pltpu.CompilerParams(vmem_limit_bytes=8 << 20),
        name="assemble",
    )(seq, one, two, ahead)


def hold_body(value_ref, *refs):
    refs[-1][...] = value_ref[...]


def hold(value, *ahead):
    near, far = pl.BlockSpec(memory_space=VMEM), pl.BlockSpec(memory_space=pl.ANY)
    return pl.pallas_call(
        hold_body,
        out_shape=jax.ShapeDtypeStruct(value.shape, value.dtype),
        in_specs=[near] + [far] * len(ahead),
        out_specs=near,
        cost_estimate=pl.CostEstimate(flops=1000, bytes_accessed=1000, transcendentals=0),
        compiler_params=pltpu.CompilerParams(vmem_limit_bytes=8 << 20),
        name="hold",
    )(value, *ahead)


def ready(cached, fresh, position, rows, tables):
    cos_ref, sin_ref, base_cos_ref, base_sin_ref = tables
    _, span, width = cached.shape
    start = rows - rows % 16
    marks = fresh[0, start:].astype(jnp.float32)[rows - start : rows - start + 1]
    token = lax.broadcasted_iota(jnp.int32, (span, width), 0).astype(jnp.float32)
    chosen = jnp.where(token == marks, 1.0, 0.0).astype(jnp.bfloat16)[:, : fresh.shape[-2]]
    keys, values = fresh[0], fresh[1]
    source = jnp.concatenate([keys, values, jnp.ones_like(keys)], 1)
    placed = jnp.dot(chosen, source, preferred_element_type=jnp.float32)
    replaced = placed[:, 2 * width :] > 0.5
    old_keys, old_values = cached[0], cached[1]
    keys = jnp.where(replaced, placed[:, :width], old_keys.astype(jnp.float32))
    values = jnp.where(replaced, placed[:, width : 2 * width], old_values.astype(jnp.float32))
    base_cos, base_sin = base_cos_ref[pl.ds(position, 1)], base_sin_ref[pl.ds(position, 1)]
    flip = jnp.where(lax.broadcasted_iota(jnp.int32, (1, width), 1) < width // 2, -1.0, 1.0)
    cosine = cos_ref[...] * base_cos - sin_ref[...] * base_sin
    sine = (sin_ref[...] * base_cos + cos_ref[...] * base_sin) * flip
    return turn(keys, cosine, sine).astype(jnp.bfloat16), values.astype(jnp.bfloat16)


def fetch(act, places, cached, fresh, cached_buf, fresh_buf, sems, position):
    for wanted, *sources in places:

        @pl.when(wanted)
        def _(sources=sources):
            for which, refs, buf in ((0, cached, cached_buf), (1, fresh, fresh_buf)):
                piece, index = sources[which]
                act(
                    pltpu.make_async_copy(
                        refs[piece].at[index], buf.at[position], sems.at[position, which]
                    )
                )


def score(query, keys):
    along = (((1,), (1,)), ((), ()))
    return lax.dot_general(query, keys, along, preferred_element_type=jnp.float32)


def absorb(first, state, scores, values, factor):
    top, mass, total = state
    before = jnp.where(first, FAR, top[...])
    after = jnp.maximum(before, jnp.max(scores, 1, keepdims=True))
    fade = jnp.where(first, 0.0, jnp.exp2((before - after) * factor))
    weight = jnp.exp2((scores - after[:, :1]) * factor)
    top[...] = after
    mass[...] = jnp.where(first, 0.0, mass[...]) * fade + jnp.sum(weight, 1, keepdims=True)
    total[...] = jnp.where(first, 0.0, total[...]) * fade + jnp.dot(
        weight.astype(jnp.bfloat16), values, preferred_element_type=jnp.float32
    )


def early_body(pieces, locate, rows, factor, slot_ref, length_ref, place_ref, seq_ref, *refs):
    cached, fresh, refs = refs[:pieces], refs[pieces : 2 * pieces], refs[2 * pieces :]
    payload_ref, query_ref, query_at_ref, query_cos_ref, query_sin_ref, *tables = refs[:9]
    turned, top, mass, total, facts, mine_ref, cached_buf, fresh_buf, keys_buf, values_buf, sems = refs[9:]
    slots, _, columns = query_ref.shape
    span, width = cached_buf.shape[-2:]
    group = columns // width
    stretches = slot_ref.shape[0]
    last = functools.reduce(jnp.maximum, [place_ref[s] for s in range(slots)])
    for slot in range(slots):
        for half in range(2):
            mine_ref[slot, half] = payload_ref[slot, half].astype(jnp.float32)[:rows].astype(jnp.bfloat16)
    chosen = far_slots(seq_ref[0], slot_ref) if pieces > 1 else []
    known = []
    for slot in chosen:
        place = place_of(slot, slot_ref)
        end = jnp.where(place >= 0, length_ref[jnp.maximum(place, 0)], 0)
        known += [jnp.where(slot >= 0, slot % 2, -1), place, end]
    known = [place_ref[slot] for slot in range(slots)] + known
    lane = lax.broadcasted_iota(jnp.int32, facts.shape, 1)
    line = jnp.zeros(facts.shape, jnp.int32)
    for k, value in enumerate(known):
        line = jnp.where(lane == k, value, line)
    facts[...] = line

    def there(position):
        places = locate(slot_ref[position], seq_ref[0], slot_ref)
        return functools.reduce(jnp.logical_or, [place[0] for place in places])

    def copies(position, act):
        places = locate(slot_ref[position], seq_ref[0], slot_ref)
        fetch(act, places, cached, fresh, cached_buf, fresh_buf, sems, position)

    def start(position, carry):
        copies(position, lambda copy: copy.start())

        @pl.when(jnp.logical_not(there(position)))
        def _():
            cached_buf[position] = jnp.zeros_like(cached_buf[position])
            fresh_buf[position] = jnp.zeros_like(fresh_buf[position])

        return carry

    lax.fori_loop(0, last + 1, start, 0)

    def prepare(slot, carry):
        @pl.when(place_ref[slot] >= 0)
        def _():
            cosine, sine = query_cos_ref[slot], query_sin_ref[slot]
            heads = [
                turn(query_ref[slot, :, h * width : (h + 1) * width].astype(jnp.float32), cosine, sine)
                for h in range(group)
            ]
            turned[slot] = jnp.concatenate(heads, 0).astype(jnp.bfloat16)

        return carry

    lax.fori_loop(0, slots, prepare, 0)
    index = lax.broadcasted_iota(jnp.int32, (rows, span), 1)

    def wall(slot, position):
        limit = query_at_ref[slot] - position * span
        limit = jnp.concatenate([limit] * (span // width), 1)
        end = jnp.where(there(position), length_ref[position] - 1, -1)
        return jnp.where(index <= jnp.minimum(limit, end), 0.0, FAR)

    if stretches <= 4:
        for count in range(1, stretches + 1):

            @pl.when(last == count - 1)
            def _(count=count):
                for position in range(count):
                    copies(position, lambda copy: copy.wait())
                for position in range(count):
                    here = slice(position * span, (position + 1) * span)
                    keys_buf[here], values_buf[here] = ready(
                        cached_buf.at[position], fresh_buf.at[position], position, rows, tables
                    )

        def one(slot, carry):
            for count in range(1, stretches + 1):

                @pl.when(place_ref[slot] == count - 1)
                def _(count=count):
                    walls = [wall(slot, position) for position in range(count)]
                    walls = jnp.concatenate([jnp.concatenate(walls, 1)] * group, 0)
                    scores = score(turned[slot], keys_buf[: count * span]) + walls
                    highest = jnp.max(scores, 1, keepdims=True)
                    weight = jnp.exp2((scores - highest) * factor)
                    shape = top.shape[1:]
                    top[slot] = jnp.broadcast_to(highest, shape)
                    mass[slot] = jnp.broadcast_to(jnp.sum(weight, 1, keepdims=True), shape)
                    total[slot] = jnp.dot(
                        weight.astype(jnp.bfloat16),
                        values_buf[: count * span],
                        preferred_element_type=jnp.float32,
                    )

            return carry

        lax.fori_loop(0, slots, one, 0)
        return

    def stretch(position, carry):
        copies(position, lambda copy: copy.wait())
        keys_buf[:span], values_buf[:span] = ready(
            cached_buf.at[position], fresh_buf.at[position], position, rows, tables
        )

        def one(slot, carry):
            @pl.when(place_ref[slot] >= position)
            def _():
                walls = jnp.concatenate([wall(slot, position)] * group, 0)
                scores = score(turned[slot], keys_buf[:span]) + walls
                state = [ref.at[slot] for ref in (top, mass, total)]
                absorb(position == 0, state, scores, values_buf[:span], factor)

            return carry

        return lax.fori_loop(0, slots, one, carry)

    lax.fori_loop(0, last + 1, stretch, 0)


def late_body(exchanged, rows, factor, *refs):
    if exchanged:
        message, fresh, *tables = refs[:6]
        refs = refs[6:]
    turned, early_top, early_mass, early_total, facts, out_ref, *refs = refs
    out_buf, keys_buf, values_buf, sems = refs
    slots, _, columns = out_buf.shape
    width = turned.shape[-1]
    group = columns // width
    mine = [facts[0, slot] for slot in range(slots)]

    def write(slot, result):
        for head in range(group):
            part = result[head * rows : (head + 1) * rows]
            out_buf[slot, :, head * width : (head + 1) * width] = part.astype(jnp.bfloat16)

    def leave(slot):
        return pltpu.make_async_copy(out_buf.at[slot], out_ref.at[slot], sems.at[slot])

    chosen = [[facts[0, slots + 3 * k + j] for j in range(3)] for k in range(2)] if exchanged else []
    touched = [
        functools.reduce(
            jnp.logical_or, [(at >= 0) & (place < mine[slot]) for at, place, _ in chosen], jnp.bool_(False)
        )
        for slot in range(slots)
    ]
    for slot in range(slots):

        @pl.when(mine[slot] < 0)
        def _(slot=slot):
            out_buf[slot] = jnp.zeros_like(out_buf[slot])
            leave(slot).start()

        @pl.when((mine[slot] >= 0) & jnp.logical_not(touched[slot]))
        def _(slot=slot):
            write(slot, early_total[slot] / early_mass[slot])
            leave(slot).start()

    def settle(slot, count):
        span = message.shape[2]
        index = lax.broadcasted_iota(jnp.int32, (1, span), 1)
        scores = []
        for k in range(count):
            _, place, length = chosen[k]
            end = jnp.where(place < mine[slot], length, 0)
            scores.append(score(turned[slot], keys_buf[k]) + jnp.where(index < end, 0.0, FAR))
        scores = jnp.concatenate(scores, 1)
        before = early_top[slot]
        after = jnp.maximum(before, jnp.max(scores, 1, keepdims=True))
        fade = jnp.exp2((before - after) * factor)
        weight = jnp.exp2((scores - after[:, :1]) * factor)
        mass = early_mass[slot] * fade + jnp.sum(weight, 1, keepdims=True)
        values = values_buf[:count].reshape(count * span, width)
        added = jnp.dot(weight.astype(jnp.bfloat16), values, preferred_element_type=jnp.float32)
        write(slot, (early_total[slot] * fade + added) / mass)

    def take(count):
        for k in range(count):
            at, place, _ = chosen[k]
            keys_buf[k], values_buf[k] = ready(message.at[at], fresh.at[at], place, rows, tables)
        for slot in range(slots):

            @pl.when(touched[slot])
            def _(slot=slot):
                settle(slot, count)
                leave(slot).start()

    if exchanged:
        pl.when((chosen[0][0] >= 0) & (chosen[1][0] < 0))(functools.partial(take, 1))
        pl.when(chosen[1][0] >= 0)(functools.partial(take, 2))
    for slot in range(slots):
        leave(slot).wait()


def attend(body, lists, far, near, out_shape, out_space, scratch, cost):
    specs = [pl.BlockSpec(memory_space=SMEM)] * len(lists)
    specs += [pl.BlockSpec(memory_space=pl.ANY)] * len(far)
    specs += [pl.BlockSpec(memory_space=VMEM)] * len(near)
    return pl.pallas_call(
        body,
        out_shape=out_shape,
        in_specs=specs,
        out_specs=jax.tree.map(lambda _: pl.BlockSpec(memory_space=out_space), out_shape),
        scratch_shapes=scratch,
        cost_estimate=pl.CostEstimate(flops=cost, bytes_accessed=1000, transcendentals=0),
        compiler_params=pltpu.CompilerParams(vmem_limit_bytes=32 << 20),
        name=body.func.__name__,
    )(*lists, *far, *near)


def locate_all(slot, seq, slot_ref):
    return [(slot >= 0, (0, slot), (0, slot))]


def locate_early(slot, seq, slot_ref):
    away, index = (slot // 2) ^ seq, slot % 2
    at_end = outer(seq)
    near = [((away == 1) & (at_end == k), (2 - k, index), (1, index)) for k in range(2)]
    next_but_one = [((away == 2) & (at_end == k), (1 + k, index), (2, index)) for k in range(2)]
    return [(away == 0, (0, index), (0, index))] + near + next_but_one


def local(
    pool_kv, hidden_rows, norm_gain, kv_weight, queries, stretch_slot, stretch_lengths, recompute_rows
):
    slots, _, span, width = pool_kv.shape
    rows = recompute_rows.shape[1]
    stretches = stretch_slot.shape[0]
    seq_count = lax.axis_size("seq")
    seq = lax.axis_index("seq")
    parts = lax.axis_size(FEATURES)
    me = lax.axis_index(FEATURES)
    features = hidden_rows.shape[2] * parts
    exchanged = seq_count == 4 and slots == 2 and stretches <= 4
    padded = round_up(rows + 1, 16)

    def along_seq(value, distance):
        return lax.ppermute(value, "seq", [(z, z ^ distance) for z in range(seq_count)])

    first, second = [(1, 3), (2, 0), (0, 1), (3, 2)], [(0, 2), (3, 1), (1, 0), (2, 3)]

    if exchanged:
        one, two = [lax.ppermute(pool_kv, "seq", pairs) for pairs in (first, second)]

    marks = jnp.pad(recompute_rows.astype(jnp.float32), ((0, 0), (0, width - rows)), constant_values=-1.0)

    def part(ks):
        return project(me.reshape(1), hidden_rows, norm_gain, kv_weight, parts, ks)

    def hand(piece, distance):
        return lax.ppermute(piece, FEATURES, [(i, i ^ distance) for i in range(parts)])

    away = tuple(range(parts - 1, 1, -1))
    sums = [hand(piece, distance) for piece, distance in zip(part(away), away)]
    near, own = part((1, 0))
    sums += [hand(near, 1), hold(own)]

    payload = finish(sums, marks, slots, rows, width, features)

    mine = seq * slots + jnp.arange(slots, dtype=jnp.int32)
    hits = stretch_slot[:, None] == mine[None]
    order = jnp.arange(stretches, dtype=jnp.int32)[:, None]
    my_pos = jnp.max(jnp.where(hits, order, -1), 0)
    query_at = my_pos[:, None] * span + recompute_rows
    inverse = THETA ** (-2.0 * np.arange(width // 2) / width)
    inverse = np.concatenate([inverse, inverse]).astype(np.float32)
    angle = query_at.astype(jnp.float32)[..., None] * inverse
    flip = np.where(np.arange(width) < width // 2, -1.0, 1.0).astype(np.float32)
    query_tables = (
        jnp.broadcast_to(query_at[..., None], (slots, rows, width)),
        jnp.cos(angle),
        jnp.sin(angle) * flip,
    )
    tables = (*rope_tables(np.arange(span), width), *rope_tables(np.arange(stretches) * span, width))

    if exchanged:
        payloads = [payload, along_seq(payload, 1), along_seq(payload, 2)]
        message = assemble(seq.reshape(1), one, two, payload)
        early, locate = ([pool_kv, one, two], payloads), locate_early
        late = (along_seq(message, 1), along_seq(hold(payloads[2], message), 1), *tables)
    else:
        early = [[lax.all_gather(array, "seq", axis=0, tiled=True)] for array in (pool_kv, payload)]
        locate, late = locate_all, ()

    lists = (stretch_slot, stretch_lengths, my_pos, seq.reshape(1))
    lines = rows * (queries.shape[2] // width)
    factor = width ** (-0.5) * math.log2(math.e)
    state = (slots, lines, width)
    stage = pltpu.VMEM(((stretches if stretches <= 4 else 1) * span, width), jnp.bfloat16)
    *passed, fresh_kv = attend(
        functools.partial(early_body, len(early[0]), locate, rows, factor),
        lists,
        (*early[0], *early[1]),
        (payload, queries, *query_tables, *tables),
        [jax.ShapeDtypeStruct(state, jnp.bfloat16)]
        + [jax.ShapeDtypeStruct(state, jnp.float32)] * 3
        + [jax.ShapeDtypeStruct((8, 128), jnp.int32)]
        + [jax.ShapeDtypeStruct((slots, 2, rows, width), jnp.bfloat16)],
        VMEM,
        [
            pltpu.VMEM((stretches, 2, span, width), jnp.bfloat16),
            pltpu.VMEM((stretches, 2, padded, width), jnp.bfloat16),
            stage,
            stage,
            pltpu.SemaphoreType.DMA((stretches, 2)),
        ],
        EARLY_COST,
    )
    attended = attend(
        functools.partial(late_body, exchanged, rows, factor),
        (),
        (),
        (*late, *passed),
        jax.ShapeDtypeStruct(queries.shape, jnp.bfloat16),
        pl.ANY,
        [
            pltpu.VMEM(queries.shape, jnp.bfloat16),
            pltpu.VMEM((2, span, width), jnp.bfloat16),
            pltpu.VMEM((2, span, width), jnp.bfloat16),
            pltpu.SemaphoreType.DMA((slots,)),
        ],
        1000,
    )
    return fresh_kv, attended


def solution(mesh):
    in_specs = (
        P(("groups", "seq"), None, None, FEATURES),
        P(("groups", "seq"), None, FEATURES),
        P(FEATURES),
        P(FEATURES, None),
        P(("groups", "seq"), None, FEATURES),
        P("groups"),
        P("groups"),
        P(("groups", "seq"), None),
    )
    out_specs = (
        P(("groups", "seq"), None, None, FEATURES),
        P(("groups", "seq"), None, FEATURES),
    )
    return jax.shard_map(local, mesh=mesh, in_specs=in_specs, out_specs=out_specs, check_vma=False)
```

```python
import functools
import math

import jax
import jax.numpy as jnp
import numpy as np
from jax import lax
from jax.experimental import pallas as pl
from jax.experimental.pallas import tpu as pltpu
from jax.sharding import PartitionSpec as P

THETA = 500000.0
EPS = 1e-05
FAR = -1e30
FEATURES = ("tp", "kvh")
VMEM = pltpu.MemorySpace.VMEM
SMEM = pltpu.MemorySpace.SMEM
PROJECT_VMEM = 61 << 20
EARLY_COST = 3*10**9


def round_up(value, step):
    return -(-value // step) * step


def rope_tables(positions, width):
    inverse = THETA ** (-2.0 * np.arange(width // 2) / width)
    angle = np.asarray(positions, np.float64)[:, None] * np.concatenate([inverse, inverse])[None]
    return np.cos(angle).astype(np.float32), np.sin(angle).astype(np.float32)


def turn(values, cosine, sine):
    return values * cosine + pltpu.roll(values, values.shape[-1] // 2, 1) * sine


def place_of(slot, slot_ref):
    place = jnp.int32(-1)
    for position in range(slot_ref.shape[0]):
        place = jnp.where(slot_ref[position] == slot, jnp.int32(position), place)
    return place


def far_slots(seq, slot_ref):
    last = jnp.maximum(*[place_of(2 * seq + j, slot_ref) for j in range(2)])
    slots = [2 * (seq ^ 3) + j for j in range(2)]
    slots = [jnp.where(place_of(slot, slot_ref) < last, slot, -1) for slot in slots]
    slots = [jnp.where(place_of(slot, slot_ref) < 0, -1, slot) for slot in slots]
    return [jnp.where(slots[0] >= 0, slots[0], slots[1]), jnp.where(slots[0] >= 0, slots[1], -1)]


def project_body(ks, me_ref, hidden_ref, gain_ref, weight_ref, *refs):
    *pieces, held, gain, weights, sems = refs
    slots, rows, features = held.shape
    count = slots * rows
    height, columns = pieces[0].shape
    spare = height - count

    def block(at, k):
        first = pl.multiple_of((me_ref[0] ^ k) * columns, columns)
        part = weight_ref.at[:, pl.ds(first, columns)]
        return pltpu.make_async_copy(part, weights.at[at], sems.at[2 + at])

    arrive = pltpu.make_async_copy(hidden_ref, held, sems.at[0])
    follow = pltpu.make_async_copy(gain_ref, gain, sems.at[1])
    arrive.start()
    follow.start()
    for at, k in enumerate(ks):
        block(at, k).start()
    arrive.wait()
    follow.wait()
    hidden = held[...].astype(jnp.float32).reshape(count, features)
    scaled = (hidden * gain[...].astype(jnp.float32).reshape(1, features)).astype(jnp.bfloat16)
    square = hidden * hidden
    fill = jnp.zeros((round_up(count, 128) - count, features), jnp.float32)
    square = jnp.concatenate([square, fill], 0)
    high = square.astype(jnp.bfloat16)
    low = (square - high.astype(jnp.float32)).astype(jnp.bfloat16)
    ones = jnp.ones((spare, features), jnp.bfloat16)
    along = (((1,), (1,)), ((), ()))
    total = lax.dot_general(ones, high, along, preferred_element_type=jnp.float32)
    total += lax.dot_general(ones, low, along, preferred_element_type=jnp.float32)
    coarse = total.astype(jnp.bfloat16).astype(jnp.float32)
    row = lax.broadcasted_iota(jnp.int32, total.shape, 0)
    both = jnp.where(row == 0, coarse, jnp.where(row == 1, total - coarse, 0.0))
    rest = jnp.zeros((spare, columns - total.shape[1]), jnp.float32)
    tail = jnp.concatenate([both, rest], 1).astype(jnp.bfloat16)
    for at, k in enumerate(ks):
        block(at, k).wait()
        product = jnp.dot(scaled, weights[at], preferred_element_type=jnp.float32)
        pieces[at][:count] = product.astype(jnp.bfloat16)
        pieces[at][count:] = tail


def project(me, hidden_rows, norm_gain, kv_weight, parts, ks):
    slots, rows, features = hidden_rows.shape
    columns = kv_weight.shape[1] // parts
    shape = (slots * rows + 16, columns)
    return pl.pallas_call(
        functools.partial(project_body, ks),
        out_shape=[jax.ShapeDtypeStruct(shape, jnp.bfloat16)] * len(ks),
        in_specs=[pl.BlockSpec(memory_space=SMEM)] + [pl.BlockSpec(memory_space=pltpu.HBM)] * 3,
        out_specs=[pl.BlockSpec(memory_space=VMEM)] * len(ks),
        scratch_shapes=[
            pltpu.VMEM(hidden_rows.shape, jnp.bfloat16),
            pltpu.VMEM(norm_gain.shape, jnp.bfloat16),
            pltpu.VMEM((len(ks), features, columns), jnp.bfloat16),
            pltpu.SemaphoreType.DMA((2 + len(ks),)),
        ],
        cost_estimate=pl.CostEstimate(flops=1000, bytes_accessed=1000, transcendentals=0),
        compiler_params=pltpu.CompilerParams(vmem_limit_bytes=PROJECT_VMEM),
        name="project",
    )(me, hidden_rows, norm_gain, kv_weight)


def finish_body(features, rows, marks_ref, *refs):
    *pieces, payload_ref = refs
    slots, _, padded, width = payload_ref.shape
    count = slots * rows
    total = pieces[0][...].astype(jnp.float32)
    for piece in pieces[1:]:
        total += piece[...].astype(jnp.float32)
    lanes = round_up(count, 128)
    squares = total[count : count + 1, :lanes] + total[count + 1 : count + 2, :lanes]
    inverse = lax.rsqrt(squares / features + EPS)
    inverse = jnp.transpose(jnp.broadcast_to(inverse, (lanes, lanes)))[:count, :width]
    for half in range(2):
        values = total[:count, half * width : (half + 1) * width] * inverse
        for slot in range(slots):
            mine = values[slot * rows : (slot + 1) * rows]
            marks = jnp.broadcast_to(marks_ref[slot : slot + 1], (padded - rows, width))
            marked = jnp.concatenate([mine, marks], 0)
            payload_ref[slot, half] = marked.astype(jnp.bfloat16)


def finish(pieces, marks, slots, rows, width, features):
    shape = (slots, 2, round_up(rows + 1, 16), width)
    return pl.pallas_call(
        functools.partial(finish_body, features, rows),
        out_shape=jax.ShapeDtypeStruct(shape, jnp.bfloat16),
        cost_estimate=pl.CostEstimate(flops=1000, bytes_accessed=1000, transcendentals=0),
        compiler_params=pltpu.CompilerParams(vmem_limit_bytes=8 << 20),
        name="finish",
    )(marks, *pieces)


def hold_body(value_ref, *refs):
    refs[-1][...] = value_ref[...]


def hold(value, *ahead):
    near, far = pl.BlockSpec(memory_space=VMEM), pl.BlockSpec(memory_space=pl.ANY)
    return pl.pallas_call(
        hold_body,
        out_shape=jax.ShapeDtypeStruct(value.shape, value.dtype),
        in_specs=[near] + [far] * len(ahead),
        out_specs=near,
        cost_estimate=pl.CostEstimate(flops=1000, bytes_accessed=1000, transcendentals=0),
        compiler_params=pltpu.CompilerParams(vmem_limit_bytes=8 << 20),
        name="hold",
    )(value, *ahead)


def ready(cached, fresh, position, rows, tables):
    cos_ref, sin_ref, base_cos_ref, base_sin_ref = tables
    _, span, width = cached.shape
    start = rows - rows % 16
    marks = fresh[0, start:].astype(jnp.float32)[rows - start : rows - start + 1]
    token = lax.broadcasted_iota(jnp.int32, (span, width), 0).astype(jnp.float32)
    chosen = jnp.where(token == marks, 1.0, 0.0).astype(jnp.bfloat16)[:, : fresh.shape[-2]]
    keys, values = fresh[0], fresh[1]
    source = jnp.concatenate([keys, values, jnp.ones_like(keys)], 1)
    placed = jnp.dot(chosen, source, preferred_element_type=jnp.float32)
    replaced = placed[:, 2 * width :] > 0.5
    old_keys, old_values = cached[0], cached[1]
    keys = jnp.where(replaced, placed[:, :width], old_keys.astype(jnp.float32))
    values = jnp.where(replaced, placed[:, width : 2 * width], old_values.astype(jnp.float32))
    base_cos, base_sin = base_cos_ref[pl.ds(position, 1)], base_sin_ref[pl.ds(position, 1)]
    flip = jnp.where(lax.broadcasted_iota(jnp.int32, (1, width), 1) < width // 2, -1.0, 1.0)
    cosine = cos_ref[...] * base_cos - sin_ref[...] * base_sin
    sine = (sin_ref[...] * base_cos + cos_ref[...] * base_sin) * flip
    return turn(keys, cosine, sine).astype(jnp.bfloat16), values.astype(jnp.bfloat16)


def fetch(act, places, cached, fresh, cached_buf, fresh_buf, sems, position):
    for wanted, *sources in places:

        @pl.when(wanted)
        def _(sources=sources):
            for which, refs, buf in ((0, cached, cached_buf), (1, fresh, fresh_buf)):
                piece, index = sources[which]
                act(
                    pltpu.make_async_copy(
                        refs[piece].at[index], buf.at[position], sems.at[position, which]
                    )
                )


def score(query, keys):
    along = (((1,), (1,)), ((), ()))
    return lax.dot_general(query, keys, along, preferred_element_type=jnp.float32)


def absorb(first, state, scores, values, factor):
    top, mass, total = state
    before = jnp.where(first, FAR, top[...])
    after = jnp.maximum(before, jnp.max(scores, 1, keepdims=True))
    fade = jnp.where(first, 0.0, jnp.exp2((before - after) * factor))
    weight = jnp.exp2((scores - after[:, :1]) * factor)
    top[...] = after
    mass[...] = jnp.where(first, 0.0, mass[...]) * fade + jnp.sum(weight, 1, keepdims=True)
    total[...] = jnp.where(first, 0.0, total[...]) * fade + jnp.dot(
        weight.astype(jnp.bfloat16), values, preferred_element_type=jnp.float32
    )


def early_body(pieces, locate, rows, factor, slot_ref, length_ref, place_ref, seq_ref, *refs):
    cached, fresh, refs = refs[:pieces], refs[pieces : 2 * pieces], refs[2 * pieces :]
    payload_ref, query_ref, query_at_ref, query_cos_ref, query_sin_ref, *tables = refs[:9]
    turned, top, mass, total, facts, mine_ref, cached_buf, fresh_buf, keys_buf, values_buf, sems = refs[9:]
    slots, _, columns = query_ref.shape
    span, width = cached_buf.shape[-2:]
    group = columns // width
    stretches = slot_ref.shape[0]
    last = functools.reduce(jnp.maximum, [place_ref[s] for s in range(slots)])
    for slot in range(slots):
        for half in range(2):
            mine_ref[slot, half] = payload_ref[slot, half].astype(jnp.float32)[:rows].astype(jnp.bfloat16)
    chosen = far_slots(seq_ref[0], slot_ref) if pieces > 1 else []
    known = []
    for slot in chosen:
        place = place_of(slot, slot_ref)
        end = jnp.where(place >= 0, length_ref[jnp.maximum(place, 0)], 0)
        known += [jnp.where(slot >= 0, slot % 2, -1), place, end]
    known = [place_ref[slot] for slot in range(slots)] + known
    lane = lax.broadcasted_iota(jnp.int32, facts.shape, 1)
    line = jnp.zeros(facts.shape, jnp.int32)
    for k, value in enumerate(known):
        line = jnp.where(lane == k, value, line)
    facts[...] = line

    def there(position):
        places = locate(slot_ref[position], seq_ref[0], slot_ref)
        return functools.reduce(jnp.logical_or, [place[0] for place in places])

    def copies(position, act):
        places = locate(slot_ref[position], seq_ref[0], slot_ref)
        fetch(act, places, cached, fresh, cached_buf, fresh_buf, sems, position)

    def start(position, carry):
        copies(position, lambda copy: copy.start())

        @pl.when(jnp.logical_not(there(position)))
        def _():
            cached_buf[position] = jnp.zeros_like(cached_buf[position])
            fresh_buf[position] = jnp.zeros_like(fresh_buf[position])

        return carry

    lax.fori_loop(0, last + 1, start, 0)

    def prepare(slot, carry):
        @pl.when(place_ref[slot] >= 0)
        def _():
            cosine, sine = query_cos_ref[slot], query_sin_ref[slot]
            heads = [
                turn(query_ref[slot, :, h * width : (h + 1) * width].astype(jnp.float32), cosine, sine)
                for h in range(group)
            ]
            turned[slot] = jnp.concatenate(heads, 0).astype(jnp.bfloat16)

        return carry

    lax.fori_loop(0, slots, prepare, 0)
    index = lax.broadcasted_iota(jnp.int32, (rows, span), 1)

    def wall(slot, position):
        limit = query_at_ref[slot] - position * span
        limit = jnp.concatenate([limit] * (span // width), 1)
        end = jnp.where(there(position), length_ref[position] - 1, -1)
        return jnp.where(index <= jnp.minimum(limit, end), 0.0, FAR)

    if stretches <= 4:
        for count in range(1, stretches + 1):

            @pl.when(last == count - 1)
            def _(count=count):
                for position in range(count):
                    copies(position, lambda copy: copy.wait())
                for position in range(count):
                    here = slice(position * span, (position + 1) * span)
                    keys_buf[here], values_buf[here] = ready(
                        cached_buf.at[position], fresh_buf.at[position], position, rows, tables
                    )

        def one(slot, carry):
            for count in range(1, stretches + 1):

                @pl.when(place_ref[slot] == count - 1)
                def _(count=count):
                    walls = [wall(slot, position) for position in range(count)]
                    walls = jnp.concatenate([jnp.concatenate(walls, 1)] * group, 0)
                    scores = score(turned[slot], keys_buf[: count * span]) + walls
                    highest = jnp.max(scores, 1, keepdims=True)
                    weight = jnp.exp2((scores - highest) * factor)
                    shape = top.shape[1:]
                    top[slot] = jnp.broadcast_to(highest, shape)
                    mass[slot] = jnp.broadcast_to(jnp.sum(weight, 1, keepdims=True), shape)
                    total[slot] = jnp.dot(
                        weight.astype(jnp.bfloat16),
                        values_buf[: count * span],
                        preferred_element_type=jnp.float32,
                    )

            return carry

        lax.fori_loop(0, slots, one, 0)
        return

    def stretch(position, carry):
        copies(position, lambda copy: copy.wait())
        keys_buf[:span], values_buf[:span] = ready(
            cached_buf.at[position], fresh_buf.at[position], position, rows, tables
        )

        def one(slot, carry):
            @pl.when(place_ref[slot] >= position)
            def _():
                walls = jnp.concatenate([wall(slot, position)] * group, 0)
                scores = score(turned[slot], keys_buf[:span]) + walls
                state = [ref.at[slot] for ref in (top, mass, total)]
                absorb(position == 0, state, scores, values_buf[:span], factor)

            return carry

        return lax.fori_loop(0, slots, one, carry)

    lax.fori_loop(0, last + 1, stretch, 0)


def late_body(exchanged, rows, factor, *refs):
    if exchanged:
        message, fresh, *tables = refs[:6]
        refs = refs[6:]
    turned, early_top, early_mass, early_total, facts, out_ref, *refs = refs
    out_buf, keys_buf, values_buf, sems = refs
    slots, _, columns = out_buf.shape
    width = turned.shape[-1]
    group = columns // width
    mine = [facts[0, slot] for slot in range(slots)]

    def write(slot, result):
        for head in range(group):
            part = result[head * rows : (head + 1) * rows]
            out_buf[slot, :, head * width : (head + 1) * width] = part.astype(jnp.bfloat16)

    def leave(slot):
        return pltpu.make_async_copy(out_buf.at[slot], out_ref.at[slot], sems.at[slot])

    chosen = [[facts[0, slots + 3 * k + j] for j in range(3)] for k in range(2)] if exchanged else []
    touched = [
        functools.reduce(
            jnp.logical_or, [(at >= 0) & (place < mine[slot]) for at, place, _ in chosen], jnp.bool_(False)
        )
        for slot in range(slots)
    ]
    for slot in range(slots):

        @pl.when(mine[slot] < 0)
        def _(slot=slot):
            out_buf[slot] = jnp.zeros_like(out_buf[slot])
            leave(slot).start()

        @pl.when((mine[slot] >= 0) & jnp.logical_not(touched[slot]))
        def _(slot=slot):
            write(slot, early_total[slot] / early_mass[slot])
            leave(slot).start()

    def settle(slot, count):
        span = message.shape[2]
        index = lax.broadcasted_iota(jnp.int32, (1, span), 1)
        scores = []
        for k in range(count):
            _, place, length = chosen[k]
            end = jnp.where(place < mine[slot], length, 0)
            scores.append(score(turned[slot], keys_buf[k]) + jnp.where(index < end, 0.0, FAR))
        scores = jnp.concatenate(scores, 1)
        before = early_top[slot]
        after = jnp.maximum(before, jnp.max(scores, 1, keepdims=True))
        fade = jnp.exp2((before - after) * factor)
        weight = jnp.exp2((scores - after[:, :1]) * factor)
        mass = early_mass[slot] * fade + jnp.sum(weight, 1, keepdims=True)
        values = values_buf[:count].reshape(count * span, width)
        added = jnp.dot(weight.astype(jnp.bfloat16), values, preferred_element_type=jnp.float32)
        write(slot, (early_total[slot] * fade + added) / mass)

    def take(count):
        for k in range(count):
            at, place, _ = chosen[k]
            keys_buf[k], values_buf[k] = ready(message.at[at], fresh.at[at], place, rows, tables)
        for slot in range(slots):

            @pl.when(touched[slot])
            def _(slot=slot):
                settle(slot, count)
                leave(slot).start()

    if exchanged:
        pl.when((chosen[0][0] >= 0) & (chosen[1][0] < 0))(functools.partial(take, 1))
        pl.when(chosen[1][0] >= 0)(functools.partial(take, 2))
    for slot in range(slots):
        leave(slot).wait()


def attend(body, lists, far, near, out_shape, out_space, scratch, cost):
    specs = [pl.BlockSpec(memory_space=SMEM)] * len(lists)
    specs += [pl.BlockSpec(memory_space=pl.ANY)] * len(far)
    specs += [pl.BlockSpec(memory_space=VMEM)] * len(near)
    return pl.pallas_call(
        body,
        out_shape=out_shape,
        in_specs=specs,
        out_specs=jax.tree.map(lambda _: pl.BlockSpec(memory_space=out_space), out_shape),
        scratch_shapes=scratch,
        cost_estimate=pl.CostEstimate(flops=cost, bytes_accessed=1000, transcendentals=0),
        compiler_params=pltpu.CompilerParams(vmem_limit_bytes=32 << 20),
        name=body.func.__name__,
    )(*lists, *far, *near)


def locate_all(slot, seq, slot_ref):
    return [(slot >= 0, (0, slot), (0, slot))]


def locate_early(slot, seq, slot_ref):
    away, index = (slot // 2) ^ seq, slot % 2
    return [(away == k, (k, index), (k, index)) for k in range(3)]


def local(
    pool_kv, hidden_rows, norm_gain, kv_weight, queries, stretch_slot, stretch_lengths, recompute_rows
):
    slots, _, span, width = pool_kv.shape
    rows = recompute_rows.shape[1]
    stretches = stretch_slot.shape[0]
    seq_count = lax.axis_size("seq")
    seq = lax.axis_index("seq")
    parts = lax.axis_size(FEATURES)
    me = lax.axis_index(FEATURES)
    features = hidden_rows.shape[2] * parts
    exchanged = seq_count == 4 and slots == 2 and stretches <= 4
    padded = round_up(rows + 1, 16)

    def along_seq(value, distance):
        return lax.ppermute(value, "seq", [(z, z ^ distance) for z in range(seq_count)])

    if exchanged:
        beside, across = along_seq(pool_kv, 1), along_seq(pool_kv, 2)

    marks = jnp.pad(recompute_rows.astype(jnp.float32), ((0, 0), (0, width - rows)), constant_values=-1.0)

    def part(ks):
        return project(me.reshape(1), hidden_rows, norm_gain, kv_weight, parts, ks)

    def hand(piece, distance):
        return lax.ppermute(piece, FEATURES, [(i, i ^ distance) for i in range(parts)])

    away = tuple(range(parts - 1, 1, -1))
    sums = [hand(piece, distance) for piece, distance in zip(part(away), away)]
    near, own = part((1, 0))
    sums += [hand(near, 1), hold(own)]

    payload = finish(sums, marks, slots, rows, width, features)

    mine = seq * slots + jnp.arange(slots, dtype=jnp.int32)
    hits = stretch_slot[:, None] == mine[None]
    order = jnp.arange(stretches, dtype=jnp.int32)[:, None]
    my_pos = jnp.max(jnp.where(hits, order, -1), 0)
    query_at = my_pos[:, None] * span + recompute_rows
    inverse = THETA ** (-2.0 * np.arange(width // 2) / width)
    inverse = np.concatenate([inverse, inverse]).astype(np.float32)
    angle = query_at.astype(jnp.float32)[..., None] * inverse
    flip = np.where(np.arange(width) < width // 2, -1.0, 1.0).astype(np.float32)
    query_tables = (
        jnp.broadcast_to(query_at[..., None], (slots, rows, width)),
        jnp.cos(angle),
        jnp.sin(angle) * flip,
    )
    tables = (*rope_tables(np.arange(span), width), *rope_tables(np.arange(stretches) * span, width))

    if exchanged:
        payloads = [payload, along_seq(payload, 1), along_seq(payload, 2)]
        message = hold(across, payload)
        early, locate = ([pool_kv, beside, across], payloads), locate_early
        late = (along_seq(message, 1), along_seq(hold(payloads[2], message), 1), *tables)
    else:
        early = [[lax.all_gather(array, "seq", axis=0, tiled=True)] for array in (pool_kv, payload)]
        locate, late = locate_all, ()

    lists = (stretch_slot, stretch_lengths, my_pos, seq.reshape(1))
    lines = rows * (queries.shape[2] // width)
    factor = width ** (-0.5) * math.log2(math.e)
    state = (slots, lines, width)
    stage = pltpu.VMEM(((stretches if stretches <= 4 else 1) * span, width), jnp.bfloat16)
    *passed, fresh_kv = attend(
        functools.partial(early_body, len(early[0]), locate, rows, factor),
        lists,
        (*early[0], *early[1]),
        (payload, queries, *query_tables, *tables),
        [jax.ShapeDtypeStruct(state, jnp.bfloat16)]
        + [jax.ShapeDtypeStruct(state, jnp.float32)] * 3
        + [jax.ShapeDtypeStruct((8, 128), jnp.int32)]
        + [jax.ShapeDtypeStruct((slots, 2, rows, width), jnp.bfloat16)],
        VMEM,
        [
            pltpu.VMEM((stretches, 2, span, width), jnp.bfloat16),
            pltpu.VMEM((stretches, 2, padded, width), jnp.bfloat16),
            stage,
            stage,
            pltpu.SemaphoreType.DMA((stretches, 2)),
        ],
        EARLY_COST,
    )
    attended = attend(
        functools.partial(late_body, exchanged, rows, factor),
        (),
        (),
        (*late, *passed),
        jax.ShapeDtypeStruct(queries.shape, jnp.bfloat16),
        pl.ANY,
        [
            pltpu.VMEM(queries.shape, jnp.bfloat16),
            pltpu.VMEM((2, span, width), jnp.bfloat16),
            pltpu.VMEM((2, span, width), jnp.bfloat16),
            pltpu.SemaphoreType.DMA((slots,)),
        ],
        1000,
    )
    return fresh_kv, attended


def solution(mesh):
    in_specs = (
        P(("groups", "seq"), None, None, FEATURES),
        P(("groups", "seq"), None, FEATURES),
        P(FEATURES),
        P(FEATURES, None),
        P(("groups", "seq"), None, FEATURES),
        P("groups"),
        P("groups"),
        P(("groups", "seq"), None),
    )
    out_specs = (
        P(("groups", "seq"), None, None, FEATURES),
        P(("groups", "seq"), None, FEATURES),
    )
    return jax.shard_map(local, mesh=mesh, in_specs=in_specs, out_specs=out_specs, check_vma=False)
```
